32 devices in a mesh: groups: 2 (over y), store: 4 (over z), tensor: 4 (over x, core).
Axes of the slice: x: 2, y: 2, z: 4, core: 2. Of those that a mesh axis runs over, the one named last changes fastest.
Arguments:
- stream: bfloat16 [1024, 4608], P(('groups', 'store')), parts along dimension 0, may hold values from -6 to 6
- input_norm_gain: bfloat16 [4608], replicated, may hold values from 0.5 to 1.5
- output_norm_gain: bfloat16 [4608], P('tensor'), may hold values from 0.5 to 1.5
- query_projection: bfloat16 [4608, 4096], P(None, 'tensor'), may hold values from -0.09375 to 0.09375
- key_value_weight: bfloat16 [4608, 2, 2048], P(None, None, 'tensor'), may hold values from -0.09375 to 0.09375
- output_projection: bfloat16 [4096, 4608], P('tensor'), may hold values from -0.09375 to 0.09375
- cached_key_value: bfloat16 [2, 1024, 16, 128, 128], P(None, ('groups', 'store'), 'tensor'), parts along dimension 1, may hold values from -900 to 900
- row_cache_length: int32 [1024], P(('groups', 'store')), parts along dimension 0, may hold values from 1 to 128, as said below
- row_adapter_index: int32 [1024], P(('groups', 'store')), parts along dimension 0, may hold values from 0 to 31, as said below
- adapter_slot_table: int32 [64], P('groups'), parts along dimension 0, may hold values from 0 to 31, as said below
- adapter_rank_table: int32 [64], P('groups'), parts along dimension 0, may hold values from 8 to 64, as said below
- adapter_down_weight: bfloat16 [4096, 64, 64], P('tensor', ('groups', 'store')), parts along dimension 1, may hold values from -0.09375 to 0.09375
- adapter_up_weight: bfloat16 [64, 64, 4608], P(('groups', 'store'), None, 'tensor'), parts along dimension 0, may hold values from -0.75 to 0.75
Outputs:
- updated: bfloat16 [1024, 4608], P(('groups', 'store'), 'tensor'), parts along dimension 0
The draws below stay inside these ranges and needn't reach their ends.
There are 2 independent parts, one for each index of `groups`. The reference program is written for one: setup_inputs(seed, part) draws one part's arguments, and reference() takes and returns one part's arrays. A program takes and returns all parts, laid end to end along the dimension named above; an argument that names none is the same for every part. Nothing has to cross between parts.
Inputs may be any that keep to these rules, and one draw needn't show every extreme that they name: `row_adapter_index`: on the rows of one store index (aligned blocks of 128 rows), at most 32 rows name adapters whose slot lies in one owner's range (adapter_slot_table[id] // 8 == owner); in every draw one owner gets exactly 32 rows from every block. `adapter_slot_table`: A permutation of the slots. `adapter_rank_table`: factor entries at rank positions from this value on are padding. `row_cache_length`: positions below this are live; the new token sits at this position.
All inputs are finite; a program needn't handle non-finite values.
Results may differ from the reference program's by a relative error of at most 0.011.
Values may be sent and summed in bfloat16 or wider, within the bound.
A program may use at most 192 MiB of HBM per device.

```python
import math
import jax
import jax.numpy as jnp
from jax import lax

MODEL_WIDTH = 4608
QUERY_HEADS = 32
KV_HEADS = 16
HEAD_WIDTH = 128
PADDED_RANK = 64
ADP_DEV = 8
ROW_DEV = 128
LC = 128
CAP = 32
ROWS = 512
ADAPTER_COUNT = 32
N_STORE = 4


def slot_table(key):
    return jax.random.permutation(jax.random.fold_in(key, 101), ADAPTER_COUNT).astype(jnp.int32)


def draw_adapter_slot_table(key, part):
    return slot_table(key)


def draw_row_adapter_index(key, part):
    table = slot_table(key)
    key = jax.random.fold_in(key, 3)
    first, second, third = jax.random.split(key, 3)
    crowded = jax.random.randint(first, (), 0, N_STORE)
    base = jnp.arange((N_STORE - 1) * CAP) // CAP
    others = (base + (base >= crowded).astype(jnp.int32)).astype(jnp.int32)

    def one_block(block_key):
        pick_key, order_key = jax.random.split(block_key)
        chosen = jax.random.permutation(pick_key, others)[:ROW_DEV - CAP]
        owners = jnp.concatenate([jnp.full((CAP,), crowded, jnp.int32), chosen.astype(jnp.int32)])
        return jax.random.permutation(order_key, owners)
    owners = jax.vmap(one_block)(jax.random.split(second, N_STORE)).reshape(ROWS)
    within = jax.random.randint(third, (ROWS,), 0, ADP_DEV)
    slots = owners * ADP_DEV + within
    inverse = jnp.argsort(table, stable=True)
    return inverse[slots].astype(jnp.int32)


def draw_adapter_rank_table(key, part):
    key = jax.random.fold_in(key, 5)
    first, second = jax.random.split(key)
    values = jax.random.randint(first, (ADAPTER_COUNT,), PADDED_RANK // 8, PADDED_RANK + 1)
    spot = jax.random.randint(second, (), 0, ADAPTER_COUNT)
    index = jnp.arange(ADAPTER_COUNT)
    values = jnp.where(index == spot, PADDED_RANK, values)
    values = jnp.where(index == (spot + 1) % ADAPTER_COUNT, PADDED_RANK // 8, values)
    return values.astype(jnp.int32)


def draw_row_cache_length(key, part):
    key = jax.random.fold_in(key, 7)
    first, second = jax.random.split(key)
    values = jax.random.randint(first, (ROWS,), 1, LC + 1)
    spot = jax.random.randint(second, (), 0, ROWS)
    values = jnp.where(jnp.arange(ROWS) == spot, LC, values)
    return values.astype(jnp.int32)


def draw_cached_key_value(key, part):
    key = jax.random.fold_in(key, 9)
    first = jax.random.fold_in(key, 0)
    base = jnp.clip(jax.random.normal(first, (2, ROWS, KV_HEADS, LC, HEAD_WIDTH), jnp.float32), -6.0, 6.0)
    return base.astype(jnp.bfloat16)


def levels(stream_key, extent, pieces, low, largest):
    loudness = 1.0
    for dim, blocks in pieces:
        steps = jax.random.uniform(jax.random.fold_in(jax.random.fold_in(stream_key, 6), dim), (blocks,), jnp.float32, low / len(pieces), largest / len(pieces))
        loudness = loudness * jnp.repeat(jnp.exp(steps), extent[dim] // blocks).reshape((-1,) + (1,) * (len(extent) - 1 - dim))
    return loudness


def normal_values(rng, dims, spread, limit, cuts=(), kind=jnp.bfloat16):
    factor_of = levels(rng, dims, cuts, -0.22, 0.18) if cuts else 1.0
    result = jax.random.normal(rng, dims, jnp.float32) * spread * factor_of
    return jnp.minimum(jnp.maximum(result, -limit), limit).astype(kind)


def setup_inputs(seed: int = 0, part: int = 0) -> dict:
    key_of = jax.random.split(jax.random.key(seed), 14)
    own_keys = jax.random.split(jax.random.fold_in(key_of[13], part), 14)
    return {
        "stream": normal_values(own_keys[0], (ROWS, MODEL_WIDTH), 1.0, 6.0, ((0, 4),)),
        "input_norm_gain": jnp.clip(1.0 + 0.1 * jax.random.normal(key_of[1], (MODEL_WIDTH,), jnp.float32), 0.5, 1.5).astype(jnp.bfloat16),
        "output_norm_gain": jnp.clip(1.0 + 0.1 * jax.random.normal(key_of[2], (MODEL_WIDTH,), jnp.float32), 0.5, 1.5).astype(jnp.bfloat16),
        "query_projection": normal_values(key_of[3], (MODEL_WIDTH, QUERY_HEADS * HEAD_WIDTH), MODEL_WIDTH ** -0.5, 0.09375, ((1, 4),)),
        "key_value_weight": normal_values(key_of[4], (MODEL_WIDTH, 2, KV_HEADS * HEAD_WIDTH), MODEL_WIDTH ** -0.5, 0.09375, ((2, 4),)),
        "output_projection": normal_values(key_of[5], (QUERY_HEADS * HEAD_WIDTH, MODEL_WIDTH), (QUERY_HEADS * HEAD_WIDTH) ** -0.5, 0.09375, ((0, 4),)),
        "cached_key_value": draw_cached_key_value(jax.random.fold_in(jax.random.fold_in(key_of[13], part), 71), part),
        "row_cache_length": draw_row_cache_length(jax.random.fold_in(jax.random.fold_in(key_of[13], part), 71), part),
        "row_adapter_index": draw_row_adapter_index(jax.random.fold_in(jax.random.fold_in(key_of[13], part), 71), part),
        "adapter_slot_table": draw_adapter_slot_table(jax.random.fold_in(jax.random.fold_in(key_of[13], part), 71), part),
        "adapter_rank_table": draw_adapter_rank_table(jax.random.fold_in(jax.random.fold_in(key_of[13], part), 71), part),
        "adapter_down_weight": normal_values(own_keys[11], (QUERY_HEADS * HEAD_WIDTH, ADAPTER_COUNT, PADDED_RANK), (QUERY_HEADS * HEAD_WIDTH) ** -0.5, 0.09375, ((0, 4), (1, 4))),
        "adapter_up_weight": normal_values(own_keys[12], (ADAPTER_COUNT, PADDED_RANK, MODEL_WIDTH), PADDED_RANK ** -0.5, 0.75, ((0, 4), (2, 4))),
    }


epsilon = 1e-06
adapter_strength = 32.0
query_factor = 144.0 ** (-0.5)
rope_base = 10000.0

def normed_rows(values, gain):
    mean = lax.optimization_barrier(jnp.mean(values * values, axis=-1, keepdims=True))
    return values * lax.rsqrt(mean + epsilon) * gain

def rotate(values, position):
    half = values.shape[-1] // 2
    freq = jnp.exp(jnp.arange(half, dtype=jnp.float32) * (-2.0 * math.log(rope_base) / values.shape[-1]))
    angle = position.astype(jnp.float32)[:, None] * freq[None, :]
    cosine = jnp.cos(angle)[:, None, :]
    sine = jnp.sin(angle)[:, None, :]
    first = values[..., :half]
    second = values[..., half:]
    return jnp.concatenate([first * cosine - second * sine, second * cosine + first * sine], axis=-1)

def attend(query, key_new, value_new, keys, values, row_cache_length):
    query_f = query.astype(jnp.float32)
    scores = jnp.einsum('bgrd,bgld->bgrl', query_f, keys.astype(jnp.float32)) * query_factor
    own = jnp.einsum('bgrd,bgd->bgr', query_f, key_new.astype(jnp.float32)) * query_factor
    valid = jnp.arange(keys.shape[2])[None, :] < row_cache_length[:, None]
    scores = jnp.where(valid[:, None, None, :], scores, -jnp.inf)
    top = jnp.maximum(lax.optimization_barrier(jnp.max(scores, axis=-1)), own)
    weights = jnp.exp(scores - top[..., None])
    own_weight = jnp.exp(own - top)
    total = lax.optimization_barrier(jnp.sum(weights, axis=-1)) + own_weight
    probs = (weights / total[..., None]).astype(jnp.bfloat16)
    own_prob = (own_weight / total).astype(jnp.bfloat16)
    mixed = jnp.einsum('bgrl,bgld->bgrd', probs.astype(jnp.float32), values.astype(jnp.float32))
    mixed = mixed + own_prob.astype(jnp.float32)[..., None] * value_new.astype(jnp.float32)[:, :, None, :]
    return mixed.astype(jnp.bfloat16).reshape(query.shape[0], -1)

def reference(stream, input_norm_gain, output_norm_gain, query_projection, key_value_weight, output_projection, cached_key_value, row_cache_length, row_adapter_index, adapter_slot_table, adapter_rank_table, adapter_down_weight, adapter_up_weight):
    stream_f = stream.astype(jnp.float32)
    normed = normed_rows(stream_f, input_norm_gain.astype(jnp.float32)).astype(jnp.bfloat16)
    group = QUERY_HEADS // KV_HEADS
    query = jnp.dot(normed, query_projection, preferred_element_type=jnp.float32).reshape(ROWS, QUERY_HEADS, HEAD_WIDTH)
    query = rotate(query, row_cache_length).astype(jnp.bfloat16).reshape(ROWS, KV_HEADS, group, HEAD_WIDTH)
    pair = jnp.dot(normed, key_value_weight.reshape(MODEL_WIDTH, 2 * KV_HEADS * HEAD_WIDTH), preferred_element_type=jnp.float32)
    pair = pair.reshape(ROWS, 2, KV_HEADS, HEAD_WIDTH)
    key_new = rotate(pair[:, 0], row_cache_length).astype(jnp.bfloat16)
    value_new = pair[:, 1].astype(jnp.bfloat16)
    keys = cached_key_value[0]
    values = cached_key_value[1]

    def one_block(items):
        return attend(*items)
    blocked = (query.reshape(N_STORE, ROW_DEV, KV_HEADS, group, HEAD_WIDTH), key_new.reshape(N_STORE, ROW_DEV, KV_HEADS, HEAD_WIDTH), value_new.reshape(N_STORE, ROW_DEV, KV_HEADS, HEAD_WIDTH), keys.reshape(N_STORE, ROW_DEV, KV_HEADS, LC, HEAD_WIDTH), values.reshape(N_STORE, ROW_DEV, KV_HEADS, LC, HEAD_WIDTH), row_cache_length.reshape(N_STORE, ROW_DEV))
    mixed = lax.map(one_block, blocked).reshape(ROWS, QUERY_HEADS * HEAD_WIDTH)
    slot = adapter_slot_table[row_adapter_index]
    adapter_rank_value = adapter_rank_table[row_adapter_index]
    choose = (slot[:, None] == jnp.arange(ADAPTER_COUNT)[None, :]).astype(jnp.float32)
    down_factor = adapter_down_weight.reshape(QUERY_HEADS * HEAD_WIDTH, ADAPTER_COUNT * PADDED_RANK)
    gather_places = jnp.dot(mixed, down_factor, preferred_element_type=jnp.float32).reshape(ROWS, ADAPTER_COUNT, PADDED_RANK)
    gather_places = lax.optimization_barrier(jnp.sum(gather_places * choose[:, :, None], axis=1))
    live_positions = (jnp.arange(PADDED_RANK)[None, :] < adapter_rank_value[:, None]).astype(jnp.float32)
    narrow_input = (gather_places * live_positions * (adapter_strength / adapter_rank_value.astype(jnp.float32))[:, None]).astype(jnp.bfloat16)
    rank_spread = (narrow_input[:, None, :] * choose.astype(jnp.bfloat16)[:, :, None]).reshape(ROWS, ADAPTER_COUNT * PADDED_RANK)
    narrow_output = jnp.dot(rank_spread, adapter_up_weight.reshape(ADAPTER_COUNT * PADDED_RANK, MODEL_WIDTH), preferred_element_type=jnp.float32).astype(jnp.bfloat16)
    projected = jnp.dot(mixed, output_projection, preferred_element_type=jnp.float32) + narrow_output.astype(jnp.float32)
    return (stream_f + normed_rows(projected, output_norm_gain.astype(jnp.float32))).astype(jnp.bfloat16)
```

```python
import functools
import math

import jax
import jax.numpy as jnp
from jax import lax
from jax.experimental import pallas as pl
from jax.experimental.pallas import tpu as pltpu
from jax.sharding import PartitionSpec as P

MESH = pl.DeviceIdType.MESH

HEAD_WIDTH = 128


epsilon = 1e-06
adapter_strength = 32.0
query_factor = 144.0 ** (-0.5)
rope_base = 10000.0


def normed_rows(values, gain):
    mean = jnp.mean(values * values, axis=-1, keepdims=True)
    return values * lax.rsqrt(mean + epsilon) * gain


def rotate(values, position):
    half = values.shape[-1] // 2
    freq = jnp.exp(
        jnp.arange(half, dtype=jnp.float32) * (-2.0 * math.log(rope_base) / values.shape[-1])
    )
    angle = position.astype(jnp.float32)[:, None] * freq[None, :]
    cosine = jnp.cos(angle)[:, None, :]
    sine = jnp.sin(angle)[:, None, :]
    first = values[..., :half]
    second = values[..., half:]
    return jnp.concatenate(
        [first * cosine - second * sine, second * cosine + first * sine], axis=-1
    )


def attend(query, key_new, value_new, keys, values, row_cache_length):
    scores = (
        jnp.einsum("bgrd,bgld->bgrl", query, keys, preferred_element_type=jnp.float32)
        * query_factor
    )
    own = (
        jnp.einsum("bgrd,bgd->bgr", query, key_new, preferred_element_type=jnp.float32)
        * query_factor
    )
    valid = jnp.arange(keys.shape[2])[None, :] < row_cache_length[:, None]
    scores = jnp.where(valid[:, None, None, :], scores, -jnp.inf)
    top = jnp.maximum(jnp.max(scores, axis=-1), own)
    weights = jnp.exp(scores - top[..., None])
    own_weight = jnp.exp(own - top)
    total = jnp.sum(weights, axis=-1) + own_weight
    probs = (weights / total[..., None]).astype(jnp.bfloat16)
    own_prob = (own_weight / total).astype(jnp.bfloat16)
    mixed = jnp.einsum("bgrl,bgld->bgrd", probs, values, preferred_element_type=jnp.float32)
    mixed = (
        mixed
        + own_prob.astype(jnp.float32)[..., None] * value_new.astype(jnp.float32)[:, :, None, :]
    )
    return mixed.astype(jnp.bfloat16).reshape(query.shape[0], -1)


NT = (((1,), (1,)), ((), ()))
TN = (((0,), (0,)), ((), ()))


def exchange_kernel(
    stores,
    column_count,
    kept,
    capacity,
    mixed_ref,
    index_ref,
    slot_ref,
    rank_ref,
    down_ref,
    up_ref,
    gain_ref,
    stream_ref,
    weight_ref,
    out_ref,
    weight_buf,
    stream_buf,
    out_buf,
    in_buf,
    part_buf,
    part_in,
    cross_buf,
    cross_in,
    low_buf,
    low_in,
    back_buf,
    back_in,
    stat_buf,
    stat_in,
    load_sem,
    row_send,
    row_recv,
    part_send,
    part_recv,
    low_send,
    low_recv,
    back_send,
    back_recv,
    stat_send,
    stat_recv,
):
    rows, depth = mixed_ref.shape
    portion = gain_ref.shape[1]
    rank_width = down_ref.shape[0] // kept
    width = portion * column_count
    f32 = jnp.float32
    bf16 = jnp.bfloat16
    store = lax.axis_index("store")
    column = lax.axis_index("tensor")
    chip = column // 2
    core = column % 2
    chunks = [(1 - chip) * 2 + 1 - core, chip * 2 + 1 - core, (1 - chip) * 2 + core, column]
    partner = chip * 2 + 1 - core
    across = (1 - chip) * 2 + core

    loads = []
    for i, chunk in enumerate(chunks):
        start = pl.multiple_of(chunk * portion, 128)
        loads.append(
            pltpu.make_async_copy(
                weight_ref.at[:, pl.ds(start, portion)], weight_buf.at[i], load_sem.at[i]
            )
        )
    mine = pl.multiple_of(column * portion, 128)
    loads.append(
        pltpu.make_async_copy(
            stream_ref.at[:, pl.ds(mine, portion)], stream_buf, load_sem.at[column_count]
        )
    )
    for load in loads:
        load.start()

    barrier = pltpu.get_barrier_semaphore()
    for k in range(1, stores):
        pl.semaphore_signal(
            barrier, inc=1, device_id={"store": (store + k) % stores}, device_id_type=MESH
        )
    for k in range(1, column_count):
        pl.semaphore_signal(
            barrier, inc=1, device_id={"tensor": (column + k) % column_count}, device_id_type=MESH
        )

    adapters = slot_ref.shape[1]
    match = (
        lax.broadcasted_iota(jnp.int32, (adapters, rows), 0) == index_ref[...]
    ).astype(f32)
    slot = jnp.dot(
        jnp.broadcast_to(slot_ref[...].astype(f32), (8, adapters)), match, preferred_element_type=f32
    )
    rank = jnp.dot(
        jnp.broadcast_to(rank_ref[...].astype(f32), (8, adapters)), match, preferred_element_type=f32
    )
    owner = jnp.zeros((8, rows), f32)
    for s in range(1, stores):
        owner = owner + (slot >= float(s * kept)).astype(f32)
    within = slot - owner * float(kept)
    turned = owner - store.astype(f32)
    turned = jnp.where(turned < 0.0, turned + float(stores), turned)
    target = (lax.broadcasted_iota(jnp.int32, (8, rows), 0).astype(f32) == turned).astype(f32)
    earlier = (
        lax.broadcasted_iota(jnp.int32, (rows, rows), 0)
        < lax.broadcasted_iota(jnp.int32, (rows, rows), 1)
    ).astype(f32)
    before = jnp.dot(target, earlier, preferred_element_type=f32)
    place = jnp.sum(before * target, axis=0, keepdims=True) + turned[0:1] * float(capacity)
    packer_f = (
        lax.broadcasted_iota(jnp.int32, (stores * capacity, rows), 0).astype(f32) == place
    ).astype(f32)
    packer = packer_f.astype(bf16)
    line = lax.broadcasted_iota(jnp.int32, (128, rows), 0)
    labels = jnp.where(line == 0, within[0:1] + 1.0, jnp.where(line == 1, rank[0:1], 0.0))
    labels = lax.dot_general(packer, labels.astype(bf16), NT, preferred_element_type=f32)
    mixed = mixed_ref[...]
    outgoing = jnp.dot(packer, mixed, preferred_element_type=f32)
    out_buf[:, :, 0:depth] = outgoing.astype(bf16).reshape(stores, capacity, depth)
    out_buf[:, :, depth : depth + 128] = labels.astype(bf16).reshape(stores, capacity, 128)

    pl.semaphore_wait(barrier, stores + column_count - 2)

    def row_copy(k):
        return pltpu.make_async_remote_copy(
            src_ref=out_buf.at[k],
            dst_ref=in_buf.at[k - 1],
            send_sem=row_send.at[k - 1],
            recv_sem=row_recv.at[k - 1],
            device_id={"store": (store + k) % stores},
            device_id_type=MESH,
        )

    row_copies = [row_copy(k) for k in range(1, stores)]
    for copy in row_copies:
        copy.start()

    part_copies = []
    for i in range(2):
        loads[i].wait()
        part_buf[i] = jnp.dot(mixed, weight_buf[i], preferred_element_type=f32).astype(bf16)
        copy = pltpu.make_async_remote_copy(
            src_ref=part_buf.at[i],
            dst_ref=part_in.at[i],
            send_sem=part_send.at[i],
            recv_sem=part_recv.at[i],
            device_id={"tensor": partner},
            device_id_type=MESH,
        )
        copy.start()
        part_copies.append(copy)
    loads[2].wait()
    crossing = jnp.dot(mixed, weight_buf[2], preferred_element_type=f32)
    part_copies[0].wait()
    cross_buf[...] = (crossing + part_in[0].astype(f32)).astype(bf16)
    cross_copy = pltpu.make_async_remote_copy(
        src_ref=cross_buf,
        dst_ref=cross_in,
        send_sem=part_send.at[2],
        recv_sem=part_recv.at[2],
        device_id={"tensor": across},
        device_id_type=MESH,
    )
    cross_copy.start()

    for copy in row_copies:
        copy.wait()
    block = jnp.concatenate([out_buf[0]] + [in_buf[k] for k in range(stores - 1)], axis=0)
    code = block[:, depth : depth + 1].astype(f32)
    row_rank = block[:, depth + 1 : depth + 2].astype(f32)
    full = lax.dot_general(block[:, 0:depth], down_ref[...], NT, preferred_element_type=f32)
    count = stores * capacity
    lane = lax.broadcasted_iota(jnp.int32, (count, kept * rank_width), 1).astype(f32)
    choose = jnp.logical_and(
        lane >= (code - 1.0) * float(rank_width), lane < code * float(rank_width)
    )
    full = jnp.where(choose, full, 0.0)
    coordinates = full[:, 0:128]
    for i in range(1, kept * rank_width // 128):
        coordinates = coordinates + full[:, i * 128 : (i + 1) * 128]
    low_buf[...] = coordinates.astype(bf16)
    low_copies = []
    for k in range(1, column_count):
        copy = pltpu.make_async_remote_copy(
            src_ref=low_buf,
            dst_ref=low_in.at[k - 1],
            send_sem=low_send.at[k - 1],
            recv_sem=low_recv.at[k - 1],
            device_id={"tensor": (column + k) % column_count},
            device_id_type=MESH,
        )
        copy.start()
        low_copies.append(copy)

    loads[3].wait()
    own = jnp.dot(mixed, weight_buf[3], preferred_element_type=f32)
    part_copies[1].wait()
    own = own + part_in[1].astype(f32)

    for k in range(column_count - 1):
        low_copies[k].wait()
        coordinates = coordinates + low_in[k].astype(f32)
    place_in_rank = lax.broadcasted_iota(jnp.int32, (count, 128), 1) % rank_width
    live = place_in_rank.astype(f32) < row_rank
    narrow = jnp.where(live, coordinates * (adapter_strength / jnp.maximum(row_rank, 1.0)), 0.0)
    spread = jnp.concatenate([narrow] * (kept * rank_width // 128), axis=1)
    spread = jnp.where(choose, spread, 0.0).astype(bf16)
    wide = jnp.dot(spread, up_ref[...], preferred_element_type=f32).astype(bf16)
    back_buf[...] = wide.reshape(stores, capacity, portion)
    back_copies = []
    for k in range(1, stores):
        copy = pltpu.make_async_remote_copy(
            src_ref=back_buf.at[k],
            dst_ref=back_in.at[k - 1],
            send_sem=back_send.at[k - 1],
            recv_sem=back_recv.at[k - 1],
            device_id={"store": (store + stores - k) % stores},
            device_id_type=MESH,
        )
        copy.start()
        back_copies.append(copy)

    unpacker = packer_f.T.astype(bf16)
    cross_copy.wait()
    own = own + cross_in[...].astype(f32)
    for copy in back_copies:
        copy.wait()
    returned = jnp.concatenate([back_buf[0]] + [back_in[k] for k in range(stores - 1)], axis=0)
    projected = own + jnp.dot(unpacker, returned, preferred_element_type=f32)

    squares = jnp.sum(projected * projected, axis=1, keepdims=True)
    stat_buf[...] = jnp.broadcast_to(squares, (rows, 128)).T[0:8]
    stat_copies = []
    for k in range(1, column_count):
        copy = pltpu.make_async_remote_copy(
            src_ref=stat_buf,
            dst_ref=stat_in.at[k - 1],
            send_sem=stat_send.at[k - 1],
            recv_sem=stat_recv.at[k - 1],
            device_id={"tensor": (column + k) % column_count},
            device_id_type=MESH,
        )
        copy.start()
        stat_copies.append(copy)
    loads[4].wait()
    total = stat_buf[0:1]
    for k in range(column_count - 1):
        stat_copies[k].wait()
        total = total + stat_in[k, 0:1]
    total = jnp.broadcast_to(total, (128, rows)).T[:, 0:1]
    factor = lax.rsqrt(total * (1.0 / width) + epsilon)
    out_ref[...] = (
        stream_buf[...].astype(f32) + projected * factor * gain_ref[...].astype(f32)
    ).astype(bf16)


def exchange(mixed, index, slots, ranks, down, up, gain, stream, weight):
    stores = lax.axis_size("store")
    column_count = lax.axis_size("tensor")
    rows, depth = mixed.shape
    kept = down.shape[1]
    rank_width = down.shape[2]
    portion = up.shape[2]
    capacity = rows // 4
    down = jnp.transpose(down, (1, 2, 0)).reshape(kept * rank_width, depth)
    up = up.reshape(kept * rank_width, portion)
    bf16 = jnp.bfloat16
    dma = pltpu.SemaphoreType.DMA
    vmem = pl.BlockSpec(memory_space=pltpu.VMEM)
    hbm = pl.BlockSpec(memory_space=pl.ANY)
    return pl.pallas_call(
        functools.partial(exchange_kernel, stores, column_count, kept, capacity),
        out_shape=jax.ShapeDtypeStruct((rows, portion), bf16),
        in_specs=[vmem] * 7 + [hbm] * 2,
        out_specs=vmem,
        scratch_shapes=[
            pltpu.VMEM((column_count, depth, portion), bf16),
            pltpu.VMEM((rows, portion), bf16),
            pltpu.VMEM((stores, capacity, depth + 128), bf16),
            pltpu.VMEM((stores - 1, capacity, depth + 128), bf16),
            pltpu.VMEM((2, rows, portion), bf16),
            pltpu.VMEM((2, rows, portion), bf16),
            pltpu.VMEM((rows, portion), bf16),
            pltpu.VMEM((rows, portion), bf16),
            pltpu.VMEM((stores * capacity, 128), bf16),
            pltpu.VMEM((column_count - 1, stores * capacity, 128), bf16),
            pltpu.VMEM((stores, capacity, portion), bf16),
            pltpu.VMEM((stores - 1, capacity, portion), bf16),
            pltpu.VMEM((8, rows), jnp.float32),
            pltpu.VMEM((column_count - 1, 8, rows), jnp.float32),
            dma((column_count + 1,)),
            dma((stores - 1,)),
            dma((stores - 1,)),
            dma((3,)),
            dma((3,)),
            dma((column_count - 1,)),
            dma((column_count - 1,)),
            dma((stores - 1,)),
            dma((stores - 1,)),
            dma((column_count - 1,)),
            dma((column_count - 1,)),
        ],
        compiler_params=pltpu.CompilerParams(
            collective_id=0, has_side_effects=True, vmem_limit_bytes=40 << 20
        ),
    )(
        mixed,
        index.reshape(1, -1),
        slots.reshape(1, -1),
        ranks.reshape(1, -1),
        down,
        up,
        gain.reshape(1, -1),
        stream,
        weight,
    )


def per_device(
    stream,
    input_norm_gain,
    output_norm_gain,
    query_projection,
    key_value_weight,
    output_projection,
    cached_key_value,
    row_cache_length,
    row_adapter_index,
    adapter_slot_table,
    adapter_rank_table,
    adapter_down_weight,
    adapter_up_weight,
):
    stores = lax.axis_size("store")
    column = lax.axis_index("tensor")
    row_count, width = stream.shape
    kept_factors = adapter_down_weight.shape[1]
    rank_padding = adapter_down_weight.shape[2]
    adapter_portion = adapter_up_weight.shape[2]
    capacity = row_count // 4
    heads_local = query_projection.shape[1] // HEAD_WIDTH
    pairs_local = key_value_weight.shape[2] // HEAD_WIDTH
    stream_f = stream.astype(jnp.float32)
    normed = normed_rows(stream_f, input_norm_gain.astype(jnp.float32)).astype(jnp.bfloat16)
    query = jnp.dot(normed, query_projection, preferred_element_type=jnp.float32).reshape(
        row_count, heads_local, HEAD_WIDTH
    )
    query = rotate(query, row_cache_length).astype(jnp.bfloat16)
    query = query.reshape(row_count, pairs_local, heads_local // pairs_local, HEAD_WIDTH)
    pair = jnp.dot(normed, key_value_weight.reshape(width, -1), preferred_element_type=jnp.float32)
    pair = pair.reshape(row_count, 2, pairs_local, HEAD_WIDTH)
    key_new = rotate(pair[:, 0], row_cache_length).astype(jnp.bfloat16)
    value_new = pair[:, 1].astype(jnp.bfloat16)
    mixed = attend(
        query, key_new, value_new, cached_key_value[0], cached_key_value[1], row_cache_length
    )
    if lax.axis_size("tensor") == 4 and adapter_portion % 128 == 0 and row_count == 128:
        return exchange(
            mixed,
            row_adapter_index,
            adapter_slot_table,
            adapter_rank_table,
            adapter_down_weight,
            adapter_up_weight,
            output_norm_gain,
            stream,
            output_projection,
        )
    adapters = adapter_slot_table.shape[0]
    match = row_adapter_index[:, None] == jnp.arange(adapters)[None, :]
    slot = jnp.sum(jnp.where(match, adapter_slot_table[None, :], 0), axis=1)
    adapter_rank_value = jnp.sum(jnp.where(match, adapter_rank_table[None, :], 0), axis=1)
    owner = slot // kept_factors
    within = slot - owner * kept_factors
    target = (owner[:, None] == jnp.arange(stores)[None, :]).astype(jnp.int32)
    before = jnp.cumsum(target, axis=0) - target
    bucket = owner * capacity + jnp.sum(before * target, axis=1)
    packer = (bucket[None, :] == jnp.arange(stores * capacity)[:, None]).astype(jnp.bfloat16)
    outgoing = jnp.dot(packer, mixed, preferred_element_type=jnp.float32).astype(jnp.bfloat16)
    outgoing = outgoing.reshape(stores, capacity, -1)
    labels = jnp.stack(
        [(within + 1).astype(jnp.float32), adapter_rank_value.astype(jnp.float32)], axis=-1
    )
    labels = (
        jnp.dot(packer.astype(jnp.float32), labels)
        .astype(jnp.bfloat16)
        .reshape(stores, capacity, 2)
    )
    down_factor = adapter_down_weight.reshape(
        adapter_down_weight.shape[0], kept_factors * rank_padding
    )
    up_factor = adapter_up_weight.reshape(kept_factors * rank_padding, adapter_portion)
    block = lax.all_to_all(outgoing, "store", split_axis=0, concat_axis=0, tiled=True)
    marks = lax.all_to_all(labels, "store", split_axis=0, concat_axis=0, tiled=True)
    count = block.shape[0] * block.shape[1]
    flat = block.reshape(count, -1)
    code = marks[..., 0].reshape(count).astype(jnp.float32)
    row_rank_value = marks[..., 1].reshape(count).astype(jnp.float32)
    choose = code[:, None] - 1.0 == jnp.arange(kept_factors, dtype=jnp.float32)[None, :]
    gather_places = jnp.dot(flat, down_factor, preferred_element_type=jnp.float32).reshape(
        count, kept_factors, rank_padding
    )
    gather_places = jnp.sum(gather_places * choose.astype(jnp.float32)[:, :, None], axis=1)
    gather_places = lax.psum(gather_places, "tensor")
    live_positions = (
        jnp.arange(rank_padding, dtype=jnp.float32)[None, :] < row_rank_value[:, None]
    ).astype(jnp.float32)
    narrow_input = (
        gather_places
        * live_positions
        * (adapter_strength / jnp.maximum(row_rank_value, 1.0))[:, None]
    ).astype(jnp.bfloat16)
    rank_spread = (narrow_input[:, None, :] * choose.astype(jnp.bfloat16)[:, :, None]).reshape(
        count, kept_factors * rank_padding
    )
    narrow_output = jnp.dot(rank_spread, up_factor, preferred_element_type=jnp.float32).astype(
        jnp.bfloat16
    )
    narrow_output = narrow_output.reshape(block.shape[0], block.shape[1], adapter_portion)
    returned = lax.all_to_all(narrow_output, "store", split_axis=0, concat_axis=0, tiled=True)
    low_home = lax.dot_general(
        packer,
        returned.reshape(stores * capacity, adapter_portion),
        (((0,), (0,)), ((), ())),
        preferred_element_type=jnp.float32,
    )
    partial_sum = jnp.dot(mixed, output_projection, preferred_element_type=jnp.float32)
    gain = output_norm_gain.astype(jnp.float32)
    stream_mine = lax.dynamic_slice_in_dim(stream_f, column * adapter_portion, adapter_portion, 1)
    piece = (
        lax.dynamic_slice_in_dim(partial_sum, column * adapter_portion, adapter_portion, 1)
        + low_home
    )
    summand = lax.dynamic_update_slice_in_dim(partial_sum, piece, column * adapter_portion, 1)
    projected = lax.psum(summand, "tensor")
    mean = jnp.mean(projected * projected, axis=-1, keepdims=True)
    mine = lax.dynamic_slice_in_dim(projected, column * adapter_portion, adapter_portion, 1)
    return (stream_mine + mine * lax.rsqrt(mean + epsilon) * gain).astype(jnp.bfloat16)


def solution(mesh):
    in_specs = (
        P(("groups", "store"), None),
        P(),
        P("tensor"),
        P(None, "tensor"),
        P(None, None, "tensor"),
        P("tensor", None),
        P(None, ("groups", "store"), "tensor", None, None),
        P(("groups", "store")),
        P(("groups", "store")),
        P("groups"),
        P("groups"),
        P("tensor", ("groups", "store"), None),
        P(("groups", "store"), None, "tensor"),
    )
    out_specs = P(("groups", "store"), "tensor")
    return jax.shard_map(
        per_device, mesh=mesh, in_specs=in_specs, out_specs=out_specs, check_vma=False
    )
```

```python
import functools
import math

import jax
import jax.numpy as jnp
from jax import lax
from jax.experimental import pallas as pl
from jax.experimental.pallas import tpu as pltpu
from jax.sharding import PartitionSpec as P

MESH = pl.DeviceIdType.MESH
NT = (((1,), (1,)), ((), ()))

HEAD_WIDTH = 128


epsilon = 1e-06
adapter_strength = 32.0
query_factor = 144.0 ** (-0.5)
rope_base = 10000.0


def attention_kernel(
    per,
    stream_ref,
    gain_ref,
    length_ref,
    query_weight_ref,
    pair_weight_ref,
    cache_ref,
    out_ref,
    normed_buf,
    query_buf,
    pair_buf,
    cache_buf,
    query_sum,
    pair_sum,
    query_heads,
    key_heads,
    value_heads,
    length_buf,
    query_sem,
    pair_sem,
    cache_sem,
):
    rows, width = stream_ref.shape
    chunks, step, _ = query_buf.shape
    pairs = key_heads.shape[0]
    group = 128 // per
    blocks = rows // group
    parts = pairs * blocks
    octets = group // 8
    f32 = jnp.float32
    bf16 = jnp.bfloat16

    def query_copy(c):
        return pltpu.make_async_copy(
            query_weight_ref.at[pl.ds(c * step, step)], query_buf.at[c], query_sem.at[c]
        )

    def pair_copy(c):
        return pltpu.make_async_copy(
            pair_weight_ref.at[pl.ds(c * step, step)], pair_buf.at[c], pair_sem.at[c]
        )

    def cache_copy(kind, part):
        start = pl.multiple_of((part % blocks) * group, 8)
        return pltpu.make_async_copy(
            cache_ref.at[kind, pl.ds(start, group), part // blocks],
            cache_buf.at[kind, part],
            cache_sem.at[kind, part],
        )

    for c in range(chunks):
        pair_copy(c).start()
        query_copy(c).start()

    stream = stream_ref[...].astype(f32)
    scale = lax.rsqrt(jnp.mean(stream * stream, axis=-1, keepdims=True) + epsilon)
    for c in range(chunks):
        cut = slice(c * step, (c + 1) * step)
        normed_buf[c] = (stream[:, cut] * scale * gain_ref[:, cut].astype(f32)).astype(bf16)
    length = jnp.broadcast_to(length_ref[...].astype(f32), (128, rows)).T
    length_buf[...] = length
    lane = lax.broadcasted_iota(jnp.int32, (rows, 128), 1)
    exponent = (lane % 64).astype(f32) * (-2.0 * math.log(rope_base) / HEAD_WIDTH)
    angle = length * jnp.exp(exponent)
    cosine = jnp.cos(angle)
    sine = jnp.where(lane < 64, -jnp.sin(angle), jnp.sin(angle))

    near = lax.broadcasted_iota(jnp.int32, (128, 512), 0)
    far = lax.broadcasted_iota(jnp.int32, (128, 512), 1)
    spreader = (
        jnp.where(far < 256, near * 2, near * 2 + 257) == far
    ).astype(f32).astype(bf16)
    query_sum[...] = jnp.zeros_like(query_sum)
    pair_sum[...] = jnp.zeros_like(pair_sum)

    def project(c, carry):
        normed = normed_buf[c]
        wide = [
            jnp.dot(
                normed[:, i * 128 : (i + 1) * 128], spreader, preferred_element_type=f32
            ).astype(bf16)
            for i in range(step // 128)
        ]
        both = jnp.concatenate(
            [
                jnp.concatenate([w[:, :256] for w in wide], axis=1),
                jnp.concatenate([w[:, 256:] for w in wide], axis=1),
            ],
            axis=0,
        )
        pair_copy(c).wait()
        weight = pair_buf[c].reshape(2 * step, pair_buf.shape[3])
        pair_sum[...] += jnp.dot(both, weight, preferred_element_type=f32)
        query_copy(c).wait()
        query_sum[...] += jnp.dot(normed, query_buf[c], preferred_element_type=f32)

        @pl.when(c < parts)
        def _():
            cache_copy(0, c).start()
            cache_copy(1, c).start()

        return carry

    lax.fori_loop(0, chunks, project, 0)

    def turned(values):
        return values * cosine + pltpu.roll(values, 64, 1) * sine

    for h in range(pairs * per):
        query_heads[h] = turned(query_sum[:, h * 128 : (h + 1) * 128]).astype(bf16)
    for g in range(pairs):
        cut = slice(g * 128, (g + 1) * 128)
        key_heads[g] = turned(pair_sum[0:rows, cut]).astype(bf16)
        value_heads[g] = pair_sum[rows : 2 * rows, cut].astype(bf16)

    def stacked(pieces):
        return jnp.stack([p.reshape(octets, 8, 128) for p in pieces], axis=1).reshape(128, 128)

    def attend_part(part, carry):
        g = part // blocks
        start = pl.multiple_of((part % blocks) * group, 8)
        here = pl.ds(start, group)
        query = stacked([query_heads[g * per + i, here].astype(f32) for i in range(per)])
        key_new = stacked([key_heads[g, here].astype(f32)] * per)
        value_new = stacked([value_heads[g, here].astype(f32)] * per)
        limit = stacked([length_buf[here]] * per)
        own = jnp.sum(query * key_new, axis=1, keepdims=True) * query_factor
        query = query.astype(bf16)
        across = lax.broadcasted_iota(jnp.int32, (128, 128), 1)
        row_of_lane = (across // (8 * per)) * 8 + across % 8
        scores = jnp.zeros((128, 128), f32)
        cache_copy(0, part).wait()
        for j in range(octets):
            keys = cache_buf[0, part, 8 * j : 8 * j + 8].reshape(1024, 128)
            product = lax.dot_general(keys, query, NT, preferred_element_type=f32)
            for r in range(8):
                scores = jnp.where(
                    row_of_lane == 8 * j + r, product[128 * r : 128 * (r + 1)], scores
                )
        scores = scores.T * query_factor
        scores = jnp.where(across.astype(f32) < limit, scores, -jnp.inf)
        top = jnp.maximum(jnp.max(scores, axis=1, keepdims=True), own)
        weights = jnp.exp(scores - top)
        own_weight = jnp.exp(own - top)
        total = jnp.sum(weights, axis=1, keepdims=True) + own_weight
        probs = weights / total
        own_prob = (own_weight / total).astype(bf16).astype(f32)
        tall = 8 * per
        row_in_octet = lax.broadcasted_iota(jnp.int32, (tall, 128), 0) % 8
        mixed = []
        cache_copy(1, part).wait()
        for j in range(octets):
            piece = probs[tall * j : tall * (j + 1)]
            spread = jnp.concatenate(
                [jnp.where(row_in_octet == r, piece, 0.0).astype(bf16) for r in range(8)], axis=1
            )
            values = cache_buf[1, part, 8 * j : 8 * j + 8].reshape(1024, 128)
            mixed.append(jnp.dot(spread, values, preferred_element_type=f32))
        mixed = jnp.concatenate(mixed, axis=0) + own_prob * value_new
        mixed = mixed.astype(bf16).astype(f32).reshape(octets, per, 8, 128)
        for i in range(per):
            column = pl.multiple_of((g * per + i) * 128, 128)
            out_ref[here, pl.ds(column, 128)] = mixed[:, i].reshape(group, 128).astype(bf16)
        return carry

    lax.fori_loop(0, parts, attend_part, 0)


def attention(stream, gain, lengths, query_weight, pair_weight, cache):
    rows, width = stream.shape
    step = 512
    chunks = width // step
    pairs = pair_weight.shape[2] // HEAD_WIDTH
    heads = query_weight.shape[1] // HEAD_WIDTH
    per = heads // pairs
    group = 128 // per
    parts = pairs * (rows // group)
    bf16 = jnp.bfloat16
    dma = pltpu.SemaphoreType.DMA
    vmem = pl.BlockSpec(memory_space=pltpu.VMEM)
    hbm = pl.BlockSpec(memory_space=pl.ANY)
    return pl.pallas_call(
        functools.partial(attention_kernel, per),
        out_shape=jax.ShapeDtypeStruct((rows, heads * HEAD_WIDTH), bf16),
        in_specs=[vmem] * 3 + [hbm] * 3,
        out_specs=vmem,
        scratch_shapes=[
            pltpu.VMEM((chunks, rows, step), bf16),
            pltpu.VMEM((chunks, step, heads * HEAD_WIDTH), bf16),
            pltpu.VMEM((chunks, step, 2, pairs * HEAD_WIDTH), bf16),
            pltpu.VMEM((2, parts, group, cache.shape[3], HEAD_WIDTH), bf16),
            pltpu.VMEM((rows, heads * HEAD_WIDTH), jnp.float32),
            pltpu.VMEM((2 * rows, pairs * HEAD_WIDTH), jnp.float32),
            pltpu.VMEM((heads, rows, HEAD_WIDTH), bf16),
            pltpu.VMEM((pairs, rows, HEAD_WIDTH), bf16),
            pltpu.VMEM((pairs, rows, HEAD_WIDTH), bf16),
            pltpu.VMEM((rows, HEAD_WIDTH), jnp.float32),
            dma((chunks,)),
            dma((chunks,)),
            dma((2, parts)),
        ],
        compiler_params=pltpu.CompilerParams(vmem_limit_bytes=60 << 20),
    )(stream, gain.reshape(1, -1), lengths.reshape(1, -1), query_weight, pair_weight, cache)


def exchange_kernel(
    stores,
    column_count,
    kept,
    capacity,
    mixed_ref,
    index_ref,
    slot_ref,
    rank_ref,
    down_ref,
    up_ref,
    gain_ref,
    stream_ref,
    weight_ref,
    out_ref,
    weight_buf,
    stream_buf,
    out_buf,
    in_buf,
    part_buf,
    part_in,
    cross_buf,
    cross_in,
    low_buf,
    low_in,
    back_buf,
    back_in,
    stat_buf,
    stat_in,
    load_sem,
    row_send,
    row_recv,
    part_send,
    part_recv,
    low_send,
    low_recv,
    back_send,
    back_recv,
    stat_send,
    stat_recv,
):
    rows, depth = mixed_ref.shape
    portion = gain_ref.shape[1]
    rank_width = down_ref.shape[0] // kept
    width = portion * column_count
    f32 = jnp.float32
    bf16 = jnp.bfloat16
    store = lax.axis_index("store")
    column = lax.axis_index("tensor")
    chip = column // 2
    core = column % 2
    chunks = [(1 - chip) * 2 + 1 - core, chip * 2 + 1 - core, (1 - chip) * 2 + core, column]
    partner = chip * 2 + 1 - core
    across = (1 - chip) * 2 + core

    loads = []
    for i, chunk in enumerate(chunks):
        start = pl.multiple_of(chunk * portion, 128)
        loads.append(
            pltpu.make_async_copy(
                weight_ref.at[:, pl.ds(start, portion)], weight_buf.at[i], load_sem.at[i]
            )
        )
    mine = pl.multiple_of(column * portion, 128)
    loads.append(
        pltpu.make_async_copy(
            stream_ref.at[:, pl.ds(mine, portion)], stream_buf, load_sem.at[column_count]
        )
    )
    for load in loads:
        load.start()

    barrier = pltpu.get_barrier_semaphore()
    for k in range(1, stores):
        pl.semaphore_signal(
            barrier, inc=1, device_id={"store": (store + k) % stores}, device_id_type=MESH
        )
    for k in range(1, column_count):
        pl.semaphore_signal(
            barrier, inc=1, device_id={"tensor": (column + k) % column_count}, device_id_type=MESH
        )

    adapters = slot_ref.shape[1]
    match = (
        lax.broadcasted_iota(jnp.int32, (adapters, rows), 0) == index_ref[...]
    ).astype(f32)
    slot = jnp.dot(
        jnp.broadcast_to(slot_ref[...].astype(f32), (8, adapters)), match, preferred_element_type=f32
    )
    rank = jnp.dot(
        jnp.broadcast_to(rank_ref[...].astype(f32), (8, adapters)), match, preferred_element_type=f32
    )
    owner = jnp.zeros((8, rows), f32)
    for s in range(1, stores):
        owner = owner + (slot >= float(s * kept)).astype(f32)
    within = slot - owner * float(kept)
    turned = owner - store.astype(f32)
    turned = jnp.where(turned < 0.0, turned + float(stores), turned)
    target = (lax.broadcasted_iota(jnp.int32, (8, rows), 0).astype(f32) == turned).astype(f32)
    earlier = (
        lax.broadcasted_iota(jnp.int32, (rows, rows), 0)
        < lax.broadcasted_iota(jnp.int32, (rows, rows), 1)
    ).astype(f32)
    before = jnp.dot(target, earlier, preferred_element_type=f32)
    place = jnp.sum(before * target, axis=0, keepdims=True) + turned[0:1] * float(capacity)
    packer_f = (
        lax.broadcasted_iota(jnp.int32, (stores * capacity, rows), 0).astype(f32) == place
    ).astype(f32)
    packer = packer_f.astype(bf16)
    line = lax.broadcasted_iota(jnp.int32, (128, rows), 0)
    labels = jnp.where(line == 0, within[0:1] + 1.0, jnp.where(line == 1, rank[0:1], 0.0))
    labels = lax.dot_general(packer, labels.astype(bf16), NT, preferred_element_type=f32)
    mixed = mixed_ref[...]
    outgoing = jnp.dot(packer, mixed, preferred_element_type=f32)
    out_buf[:, :, 0:depth] = outgoing.astype(bf16).reshape(stores, capacity, depth)
    out_buf[:, :, depth : depth + 128] = labels.astype(bf16).reshape(stores, capacity, 128)

    pl.semaphore_wait(barrier, stores + column_count - 2)

    def row_copy(k):
        return pltpu.make_async_remote_copy(
            src_ref=out_buf.at[k],
            dst_ref=in_buf.at[k - 1],
            send_sem=row_send.at[k - 1],
            recv_sem=row_recv.at[k - 1],
            device_id={"store": (store + k) % stores},
            device_id_type=MESH,
        )

    row_copies = [row_copy(k) for k in range(1, stores)]
    for copy in row_copies:
        copy.start()

    part_copies = []
    for i in range(2):
        loads[i].wait()
        part_buf[i] = jnp.dot(mixed, weight_buf[i], preferred_element_type=f32).astype(bf16)
        copy = pltpu.make_async_remote_copy(
            src_ref=part_buf.at[i],
            dst_ref=part_in.at[i],
            send_sem=part_send.at[i],
            recv_sem=part_recv.at[i],
            device_id={"tensor": partner},
            device_id_type=MESH,
        )
        copy.start()
        part_copies.append(copy)
    loads[2].wait()
    crossing = jnp.dot(mixed, weight_buf[2], preferred_element_type=f32)
    part_copies[0].wait()
    cross_buf[...] = (crossing + part_in[0].astype(f32)).astype(bf16)
    cross_copy = pltpu.make_async_remote_copy(
        src_ref=cross_buf,
        dst_ref=cross_in,
        send_sem=part_send.at[2],
        recv_sem=part_recv.at[2],
        device_id={"tensor": across},
        device_id_type=MESH,
    )
    cross_copy.start()

    for copy in row_copies:
        copy.wait()
    block = jnp.concatenate([out_buf[0]] + [in_buf[k] for k in range(stores - 1)], axis=0)
    code = block[:, depth : depth + 1].astype(f32)
    row_rank = block[:, depth + 1 : depth + 2].astype(f32)
    full = lax.dot_general(block[:, 0:depth], down_ref[...], NT, preferred_element_type=f32)
    count = stores * capacity
    lane = lax.broadcasted_iota(jnp.int32, (count, kept * rank_width), 1).astype(f32)
    choose = jnp.logical_and(
        lane >= (code - 1.0) * float(rank_width), lane < code * float(rank_width)
    )
    full = jnp.where(choose, full, 0.0)
    coordinates = full[:, 0:128]
    for i in range(1, kept * rank_width // 128):
        coordinates = coordinates + full[:, i * 128 : (i + 1) * 128]
    low_buf[...] = coordinates.astype(bf16)
    low_copies = []
    for k in range(1, column_count):
        copy = pltpu.make_async_remote_copy(
            src_ref=low_buf,
            dst_ref=low_in.at[k - 1],
            send_sem=low_send.at[k - 1],
            recv_sem=low_recv.at[k - 1],
            device_id={"tensor": (column + k) % column_count},
            device_id_type=MESH,
        )
        copy.start()
        low_copies.append(copy)

    loads[3].wait()
    own = jnp.dot(mixed, weight_buf[3], preferred_element_type=f32)
    part_copies[1].wait()
    own = own + part_in[1].astype(f32)

    for k in range(column_count - 1):
        low_copies[k].wait()
        coordinates = coordinates + low_in[k].astype(f32)
    place_in_rank = lax.broadcasted_iota(jnp.int32, (count, 128), 1) % rank_width
    live = place_in_rank.astype(f32) < row_rank
    narrow = jnp.where(live, coordinates * (adapter_strength / jnp.maximum(row_rank, 1.0)), 0.0)
    spread = jnp.concatenate([narrow] * (kept * rank_width // 128), axis=1)
    spread = jnp.where(choose, spread, 0.0).astype(bf16)
    wide = jnp.dot(spread, up_ref[...], preferred_element_type=f32).astype(bf16)
    back_buf[...] = wide.reshape(stores, capacity, portion)
    back_copies = []
    for k in range(1, stores):
        copy = pltpu.make_async_remote_copy(
            src_ref=back_buf.at[k],
            dst_ref=back_in.at[k - 1],
            send_sem=back_send.at[k - 1],
            recv_sem=back_recv.at[k - 1],
            device_id={"store": (store + stores - k) % stores},
            device_id_type=MESH,
        )
        copy.start()
        back_copies.append(copy)

    unpacker = packer_f.T.astype(bf16)
    cross_copy.wait()
    own = own + cross_in[...].astype(f32)
    for copy in back_copies:
        copy.wait()
    returned = jnp.concatenate([back_buf[0]] + [back_in[k] for k in range(stores - 1)], axis=0)
    projected = own + jnp.dot(unpacker, returned, preferred_element_type=f32)

    squares = jnp.sum(projected * projected, axis=1, keepdims=True)
    stat_buf[...] = jnp.broadcast_to(squares, (rows, 128)).T[0:8]
    stat_copies = []
    for k in range(1, column_count):
        copy = pltpu.make_async_remote_copy(
            src_ref=stat_buf,
            dst_ref=stat_in.at[k - 1],
            send_sem=stat_send.at[k - 1],
            recv_sem=stat_recv.at[k - 1],
            device_id={"tensor": (column + k) % column_count},
            device_id_type=MESH,
        )
        copy.start()
        stat_copies.append(copy)
    loads[4].wait()
    total = stat_buf[0:1]
    for k in range(column_count - 1):
        stat_copies[k].wait()
        total = total + stat_in[k, 0:1]
    total = jnp.broadcast_to(total, (128, rows)).T[:, 0:1]
    factor = lax.rsqrt(total * (1.0 / width) + epsilon)
    out_ref[...] = (
        stream_buf[...].astype(f32) + projected * factor * gain_ref[...].astype(f32)
    ).astype(bf16)


def exchange(mixed, index, slots, ranks, down, up, gain, stream, weight):
    stores = lax.axis_size("store")
    column_count = lax.axis_size("tensor")
    rows, depth = mixed.shape
    kept = down.shape[1]
    rank_width = down.shape[2]
    portion = up.shape[2]
    capacity = rows // 4
    down = jnp.transpose(down, (1, 2, 0)).reshape(kept * rank_width, depth)
    up = up.reshape(kept * rank_width, portion)
    bf16 = jnp.bfloat16
    dma = pltpu.SemaphoreType.DMA
    vmem = pl.BlockSpec(memory_space=pltpu.VMEM)
    hbm = pl.BlockSpec(memory_space=pl.ANY)
    return pl.pallas_call(
        functools.partial(exchange_kernel, stores, column_count, kept, capacity),
        out_shape=jax.ShapeDtypeStruct((rows, portion), bf16),
        in_specs=[vmem] * 7 + [hbm] * 2,
        out_specs=vmem,
        scratch_shapes=[
            pltpu.VMEM((column_count, depth, portion), bf16),
            pltpu.VMEM((rows, portion), bf16),
            pltpu.VMEM((stores, capacity, depth + 128), bf16),
            pltpu.VMEM((stores - 1, capacity, depth + 128), bf16),
            pltpu.VMEM((2, rows, portion), bf16),
            pltpu.VMEM((2, rows, portion), bf16),
            pltpu.VMEM((rows, portion), bf16),
            pltpu.VMEM((rows, portion), bf16),
            pltpu.VMEM((stores * capacity, 128), bf16),
            pltpu.VMEM((column_count - 1, stores * capacity, 128), bf16),
            pltpu.VMEM((stores, capacity, portion), bf16),
            pltpu.VMEM((stores - 1, capacity, portion), bf16),
            pltpu.VMEM((8, rows), jnp.float32),
            pltpu.VMEM((column_count - 1, 8, rows), jnp.float32),
            dma((column_count + 1,)),
            dma((stores - 1,)),
            dma((stores - 1,)),
            dma((3,)),
            dma((3,)),
            dma((column_count - 1,)),
            dma((column_count - 1,)),
            dma((stores - 1,)),
            dma((stores - 1,)),
            dma((column_count - 1,)),
            dma((column_count - 1,)),
        ],
        compiler_params=pltpu.CompilerParams(
            collective_id=0, has_side_effects=True, vmem_limit_bytes=40 << 20
        ),
    )(
        mixed,
        index.reshape(1, -1),
        slots.reshape(1, -1),
        ranks.reshape(1, -1),
        down,
        up,
        gain.reshape(1, -1),
        stream,
        weight,
    )


def per_device(
    stream,
    input_norm_gain,
    output_norm_gain,
    query_projection,
    key_value_weight,
    output_projection,
    cached_key_value,
    row_cache_length,
    row_adapter_index,
    adapter_slot_table,
    adapter_rank_table,
    adapter_down_weight,
    adapter_up_weight,
):
    stores = lax.axis_size("store")
    column = lax.axis_index("tensor")
    row_count, width = stream.shape
    kept_factors = adapter_down_weight.shape[1]
    rank_padding = adapter_down_weight.shape[2]
    adapter_portion = adapter_up_weight.shape[2]
    capacity = row_count // 4
    mixed = attention(
        stream,
        input_norm_gain,
        row_cache_length,
        query_projection,
        key_value_weight,
        cached_key_value,
    )
    if lax.axis_size("tensor") == 4 and adapter_portion % 128 == 0 and row_count == 128:
        return exchange(
            mixed,
            row_adapter_index,
            adapter_slot_table,
            adapter_rank_table,
            adapter_down_weight,
            adapter_up_weight,
            output_norm_gain,
            stream,
            output_projection,
        )
    stream_f = stream.astype(jnp.float32)
    adapters = adapter_slot_table.shape[0]
    match = row_adapter_index[:, None] == jnp.arange(adapters)[None, :]
    slot = jnp.sum(jnp.where(match, adapter_slot_table[None, :], 0), axis=1)
    adapter_rank_value = jnp.sum(jnp.where(match, adapter_rank_table[None, :], 0), axis=1)
    owner = slot // kept_factors
    within = slot - owner * kept_factors
    target = (owner[:, None] == jnp.arange(stores)[None, :]).astype(jnp.int32)
    before = jnp.cumsum(target, axis=0) - target
    bucket = owner * capacity + jnp.sum(before * target, axis=1)
    packer = (bucket[None, :] == jnp.arange(stores * capacity)[:, None]).astype(jnp.bfloat16)
    outgoing = jnp.dot(packer, mixed, preferred_element_type=jnp.float32).astype(jnp.bfloat16)
    outgoing = outgoing.reshape(stores, capacity, -1)
    labels = jnp.stack(
        [(within + 1).astype(jnp.float32), adapter_rank_value.astype(jnp.float32)], axis=-1
    )
    labels = (
        jnp.dot(packer.astype(jnp.float32), labels)
        .astype(jnp.bfloat16)
        .reshape(stores, capacity, 2)
    )
    down_factor = adapter_down_weight.reshape(
        adapter_down_weight.shape[0], kept_factors * rank_padding
    )
    up_factor = adapter_up_weight.reshape(kept_factors * rank_padding, adapter_portion)
    block = lax.all_to_all(outgoing, "store", split_axis=0, concat_axis=0, tiled=True)
    marks = lax.all_to_all(labels, "store", split_axis=0, concat_axis=0, tiled=True)
    count = block.shape[0] * block.shape[1]
    flat = block.reshape(count, -1)
    code = marks[..., 0].reshape(count).astype(jnp.float32)
    row_rank_value = marks[..., 1].reshape(count).astype(jnp.float32)
    choose = code[:, None] - 1.0 == jnp.arange(kept_factors, dtype=jnp.float32)[None, :]
    gather_places = jnp.dot(flat, down_factor, preferred_element_type=jnp.float32).reshape(
        count, kept_factors, rank_padding
    )
    gather_places = jnp.sum(gather_places * choose.astype(jnp.float32)[:, :, None], axis=1)
    gather_places = lax.psum(gather_places, "tensor")
    live_positions = (
        jnp.arange(rank_padding, dtype=jnp.float32)[None, :] < row_rank_value[:, None]
    ).astype(jnp.float32)
    narrow_input = (
        gather_places
        * live_positions
        * (adapter_strength / jnp.maximum(row_rank_value, 1.0))[:, None]
    ).astype(jnp.bfloat16)
    rank_spread = (narrow_input[:, None, :] * choose.astype(jnp.bfloat16)[:, :, None]).reshape(
        count, kept_factors * rank_padding
    )
    narrow_output = jnp.dot(rank_spread, up_factor, preferred_element_type=jnp.float32).astype(
        jnp.bfloat16
    )
    narrow_output = narrow_output.reshape(block.shape[0], block.shape[1], adapter_portion)
    returned = lax.all_to_all(narrow_output, "store", split_axis=0, concat_axis=0, tiled=True)
    low_home = lax.dot_general(
        packer,
        returned.reshape(stores * capacity, adapter_portion),
        (((0,), (0,)), ((), ())),
        preferred_element_type=jnp.float32,
    )
    partial_sum = jnp.dot(mixed, output_projection, preferred_element_type=jnp.float32)
    gain = output_norm_gain.astype(jnp.float32)
    stream_mine = lax.dynamic_slice_in_dim(stream_f, column * adapter_portion, adapter_portion, 1)
    piece = (
        lax.dynamic_slice_in_dim(partial_sum, column * adapter_portion, adapter_portion, 1)
        + low_home
    )
    summand = lax.dynamic_update_slice_in_dim(partial_sum, piece, column * adapter_portion, 1)
    projected = lax.psum(summand, "tensor")
    mean = jnp.mean(projected * projected, axis=-1, keepdims=True)
    mine = lax.dynamic_slice_in_dim(projected, column * adapter_portion, adapter_portion, 1)
    return (stream_mine + mine * lax.rsqrt(mean + epsilon) * gain).astype(jnp.bfloat16)


def solution(mesh):
    in_specs = (
        P(("groups", "store"), None),
        P(),
        P("tensor"),
        P(None, "tensor"),
        P(None, None, "tensor"),
        P("tensor", None),
        P(None, ("groups", "store"), "tensor", None, None),
        P(("groups", "store")),
        P(("groups", "store")),
        P("groups"),
        P("groups"),
        P("tensor", ("groups", "store"), None),
        P(("groups", "store"), None, "tensor"),
    )
    out_specs = P(("groups", "store"), "tensor")
    return jax.shard_map(
        per_device, mesh=mesh, in_specs=in_specs, out_specs=out_specs, check_vma=False
    )
```

```python
import functools
import math

import jax
import jax.numpy as jnp
from jax import lax
from jax.experimental import pallas as pl
from jax.experimental.pallas import tpu as pltpu
from jax.sharding import PartitionSpec as P

MESH = pl.DeviceIdType.MESH
NT = (((1,), (1,)), ((), ()))

HEAD_WIDTH = 128


epsilon = 1e-06
adapter_strength = 32.0
query_factor = 144.0 ** (-0.5)
rope_base = 10000.0


def attention_kernel(
    per,
    begin,
    after_weights,
    after_group,
    stream_ref,
    gain_ref,
    length_ref,
    query_weight_ref,
    pair_weight_ref,
    cache_ref,
    out_ref,
    stream_buf,
    normed_buf,
    query_buf,
    pair_buf,
    cache_buf,
    query_sum,
    pair_sum,
    query_heads,
    key_heads,
    value_heads,
    length_buf,
    query_sem,
    pair_sem,
    cache_sem,
    stream_sem,
):
    rows, width = stream_buf.shape
    slots = cache_buf.shape[1]
    chunks, step, _ = query_buf.shape
    pairs = key_heads.shape[0]
    group = 128 // per
    blocks = rows // group
    parts = pairs * blocks
    octets = group // 8
    f32 = jnp.float32
    bf16 = jnp.bfloat16

    def query_copy(c):
        return pltpu.make_async_copy(
            query_weight_ref.at[pl.ds(c * step, step)], query_buf.at[c], query_sem.at[c]
        )

    def pair_copy(c):
        return pltpu.make_async_copy(
            pair_weight_ref.at[pl.ds(c * step, step)], pair_buf.at[c], pair_sem.at[c]
        )

    def cache_copy(kind, part):
        start = pl.multiple_of((part % blocks) * group, 8)
        return pltpu.make_async_copy(
            cache_ref.at[kind, pl.ds(start, group), part // blocks],
            cache_buf.at[kind, part % slots],
            cache_sem.at[kind, part % slots],
        )

    stream_copy = pltpu.make_async_copy(stream_ref, stream_buf, stream_sem)
    stream_copy.start()
    for c in range(chunks):
        pair_copy(c).start()
        query_copy(c).start()
    if begin is not None:
        begin()
    stream_copy.wait()
    stream = stream_buf[...].astype(f32)
    scale = lax.rsqrt(jnp.mean(stream * stream, axis=-1, keepdims=True) + epsilon)
    for c in range(chunks):
        cut = slice(c * step, (c + 1) * step)
        normed_buf[c] = (stream[:, cut] * scale * gain_ref[:, cut].astype(f32)).astype(bf16)
    length = jnp.broadcast_to(length_ref[...].astype(f32), (128, rows)).T
    length_buf[...] = length
    lane = lax.broadcasted_iota(jnp.int32, (rows, 128), 1)
    exponent = (lane % 64).astype(f32) * (-2.0 * math.log(rope_base) / HEAD_WIDTH)
    angle = length * jnp.exp(exponent)
    cosine = jnp.cos(angle)
    sine = jnp.where(lane < 64, -jnp.sin(angle), jnp.sin(angle))

    near = lax.broadcasted_iota(jnp.int32, (128, 512), 0)
    far = lax.broadcasted_iota(jnp.int32, (128, 512), 1)
    spreader = (
        jnp.where(far < 256, near * 2, near * 2 + 257) == far
    ).astype(f32).astype(bf16)
    query_sum[...] = jnp.zeros_like(query_sum)
    pair_sum[...] = jnp.zeros_like(pair_sum)

    def project(c, carry):
        normed = normed_buf[c]
        wide = [
            jnp.dot(
                normed[:, i * 128 : (i + 1) * 128], spreader, preferred_element_type=f32
            ).astype(bf16)
            for i in range(step // 128)
        ]
        both = jnp.concatenate(
            [
                jnp.concatenate([w[:, :256] for w in wide], axis=1),
                jnp.concatenate([w[:, 256:] for w in wide], axis=1),
            ],
            axis=0,
        )
        pair_copy(c).wait()
        weight = pair_buf[c].reshape(2 * step, pair_buf.shape[3])
        pair_sum[...] += jnp.dot(both, weight, preferred_element_type=f32)
        query_copy(c).wait()
        query_sum[...] += jnp.dot(normed, query_buf[c], preferred_element_type=f32)

        @pl.when(c < slots)
        def _():
            cache_copy(0, c).start()
            cache_copy(1, c).start()

        return carry

    lax.fori_loop(0, chunks, project, 0)
    if after_weights is not None:
        after_weights()

    def turned(values):
        return values * cosine + pltpu.roll(values, 64, 1) * sine

    for h in range(pairs * per):
        query_heads[h] = turned(query_sum[:, h * 128 : (h + 1) * 128]).astype(bf16)
    for g in range(pairs):
        cut = slice(g * 128, (g + 1) * 128)
        key_heads[g] = turned(pair_sum[0:rows, cut]).astype(bf16)
        value_heads[g] = pair_sum[rows : 2 * rows, cut].astype(bf16)

    def stacked(pieces):
        return jnp.stack([p.reshape(octets, 8, 128) for p in pieces], axis=1).reshape(128, 128)

    def attend_part(part, carry):
        g = part // blocks
        start = pl.multiple_of((part % blocks) * group, 8)
        here = pl.ds(start, group)
        query = stacked([query_heads[g * per + i, here].astype(f32) for i in range(per)])
        key_new = stacked([key_heads[g, here].astype(f32)] * per)
        value_new = stacked([value_heads[g, here].astype(f32)] * per)
        limit = stacked([length_buf[here]] * per)
        own = jnp.sum(query * key_new, axis=1, keepdims=True) * query_factor
        query = query.astype(bf16)
        across = lax.broadcasted_iota(jnp.int32, (128, 128), 1)
        row_of_lane = (across // (8 * per)) * 8 + across % 8
        scores = jnp.zeros((128, 128), f32)
        slot = part % slots
        cache_copy(0, part).wait()
        for j in range(octets):
            keys = cache_buf[0, slot, 8 * j : 8 * j + 8].reshape(1024, 128)
            product = lax.dot_general(keys, query, NT, preferred_element_type=f32)
            for r in range(8):
                scores = jnp.where(
                    row_of_lane == 8 * j + r, product[128 * r : 128 * (r + 1)], scores
                )
        scores = scores.T * query_factor
        scores = jnp.where(across.astype(f32) < limit, scores, -jnp.inf)
        top = jnp.maximum(jnp.max(scores, axis=1, keepdims=True), own)
        weights = jnp.exp(scores - top)
        own_weight = jnp.exp(own - top)
        total = jnp.sum(weights, axis=1, keepdims=True) + own_weight
        probs = weights / total
        own_prob = (own_weight / total).astype(bf16).astype(f32)
        tall = 8 * per
        row_in_octet = lax.broadcasted_iota(jnp.int32, (tall, 128), 0) % 8
        mixed = []
        cache_copy(1, part).wait()
        for j in range(octets):
            piece = probs[tall * j : tall * (j + 1)]
            spread = jnp.concatenate(
                [jnp.where(row_in_octet == r, piece, 0.0).astype(bf16) for r in range(8)], axis=1
            )
            values = cache_buf[1, slot, 8 * j : 8 * j + 8].reshape(1024, 128)
            mixed.append(jnp.dot(spread, values, preferred_element_type=f32))
        mixed = jnp.concatenate(mixed, axis=0) + own_prob * value_new
        mixed = mixed.astype(bf16).astype(f32).reshape(octets, per, 8, 128)
        for i in range(per):
            column = pl.multiple_of((g * per + i) * 128, 128)
            out_ref[here, pl.ds(column, 128)] = mixed[:, i].reshape(group, 128).astype(bf16)

        @pl.when(part + slots < parts)
        def _():
            cache_copy(0, part + slots).start()
            cache_copy(1, part + slots).start()

        if after_group is not None:

            @pl.when(part % blocks == blocks - 1)
            def _():
                after_group(g)

        return carry

    lax.fori_loop(0, parts, attend_part, 0)


def attention_scratch(rows, width, query_weight, pair_weight, cache):
    step = 512
    chunks = width // step
    pairs = pair_weight.shape[2] // HEAD_WIDTH
    heads = query_weight.shape[1] // HEAD_WIDTH
    group = 128 * pairs // heads
    slots = min(pairs * (rows // group), 5)
    bf16 = jnp.bfloat16
    dma = pltpu.SemaphoreType.DMA
    return [
        pltpu.VMEM((rows, width), bf16),
        pltpu.VMEM((chunks, rows, step), bf16),
        pltpu.VMEM((chunks, step, heads * HEAD_WIDTH), bf16),
        pltpu.VMEM((chunks, step, 2, pairs * HEAD_WIDTH), bf16),
        pltpu.VMEM((2, slots, group, cache.shape[3], HEAD_WIDTH), bf16),
        pltpu.VMEM((rows, heads * HEAD_WIDTH), jnp.float32),
        pltpu.VMEM((2 * rows, pairs * HEAD_WIDTH), jnp.float32),
        pltpu.VMEM((heads, rows, HEAD_WIDTH), bf16),
        pltpu.VMEM((pairs, rows, HEAD_WIDTH), bf16),
        pltpu.VMEM((pairs, rows, HEAD_WIDTH), bf16),
        pltpu.VMEM((rows, HEAD_WIDTH), jnp.float32),
        dma((chunks,)),
        dma((chunks,)),
        dma((2, slots)),
        dma,
    ]


def attention(stream, gain, lengths, query_weight, pair_weight, cache):
    rows, width = stream.shape
    heads = query_weight.shape[1] // HEAD_WIDTH
    per = query_weight.shape[1] // pair_weight.shape[2]
    vmem = pl.BlockSpec(memory_space=pltpu.VMEM)
    hbm = pl.BlockSpec(memory_space=pl.ANY)
    return pl.pallas_call(
        functools.partial(attention_kernel, per, None, None, None),
        out_shape=jax.ShapeDtypeStruct((rows, heads * HEAD_WIDTH), jnp.bfloat16),
        in_specs=[hbm] + [vmem] * 2 + [hbm] * 3,
        out_specs=vmem,
        scratch_shapes=attention_scratch(rows, width, query_weight, pair_weight, cache),
        compiler_params=pltpu.CompilerParams(vmem_limit_bytes=60 << 20),
    )(stream, gain.reshape(1, -1), lengths.reshape(1, -1), query_weight, pair_weight, cache)


def exchange_kernel(
    stores,
    column_count,
    kept,
    capacity,
    per,
    input_gain_ref,
    length_ref,
    index_ref,
    slot_ref,
    rank_ref,
    gain_ref,
    stream_ref,
    query_weight_ref,
    pair_weight_ref,
    cache_ref,
    down_ref,
    up_ref,
    weight_ref,
    out_ref,
    mixed_ref,
    down_buf,
    up_buf,
    packer_buf,
    weight_buf,
    stream_buf,
    out_buf,
    in_buf,
    label_buf,
    label_in,
    part_buf,
    part_in,
    cross_buf,
    cross_in,
    low_buf,
    low_in,
    back_buf,
    back_in,
    stat_buf,
    stat_in,
    load_sem,
    row_send,
    row_recv,
    label_send,
    label_recv,
    part_send,
    part_recv,
    low_send,
    low_recv,
    back_send,
    back_recv,
    stat_send,
    stat_recv,
    *attention_refs,
):
    rows, depth = mixed_ref.shape
    portion = gain_ref.shape[1]
    rank_width = down_ref.shape[0] // kept
    pairs = out_buf.shape[1]
    span = depth // pairs
    width = portion * column_count
    f32 = jnp.float32
    bf16 = jnp.bfloat16
    store = lax.axis_index("store")
    column = lax.axis_index("tensor")
    chip = column // 2
    core = column % 2
    chunks = [(1 - chip) * 2 + 1 - core, chip * 2 + 1 - core, (1 - chip) * 2 + core, column]
    partner = chip * 2 + 1 - core
    across = (1 - chip) * 2 + core

    loads = []
    for i, chunk in enumerate(chunks):
        start = pl.multiple_of(chunk * portion, 128)
        loads.append(
            pltpu.make_async_copy(
                weight_ref.at[:, pl.ds(start, portion)], weight_buf.at[i], load_sem.at[i]
            )
        )
    mine = pl.multiple_of(column * portion, 128)
    loads.append(
        pltpu.make_async_copy(
            stream_ref.at[:, pl.ds(mine, portion)], stream_buf, load_sem.at[column_count]
        )
    )
    loads.append(pltpu.make_async_copy(down_ref, down_buf, load_sem.at[column_count + 1]))
    loads.append(pltpu.make_async_copy(up_ref, up_buf, load_sem.at[column_count + 2]))

    def label_copy(k):
        return pltpu.make_async_remote_copy(
            src_ref=label_buf.at[k],
            dst_ref=label_in.at[k - 1],
            send_sem=label_send.at[k - 1],
            recv_sem=label_recv.at[k - 1],
            device_id={"store": (store + k) % stores},
            device_id_type=MESH,
        )

    def row_copy(k, g):
        return pltpu.make_async_remote_copy(
            src_ref=out_buf.at[k, g],
            dst_ref=in_buf.at[k - 1, g],
            send_sem=row_send.at[k - 1, g],
            recv_sem=row_recv.at[k - 1, g],
            device_id={"store": (store + k) % stores},
            device_id_type=MESH,
        )

    barrier = pltpu.get_barrier_semaphore()

    def begin():
        for k in range(1, stores):
            pl.semaphore_signal(
                barrier, inc=1, device_id={"store": (store + k) % stores}, device_id_type=MESH
            )
        for k in range(1, column_count):
            pl.semaphore_signal(
                barrier, inc=1, device_id={"tensor": (column + k) % column_count}, device_id_type=MESH
            )

        adapters = slot_ref.shape[1]
        match = (
            lax.broadcasted_iota(jnp.int32, (adapters, rows), 0) == index_ref[...]
        ).astype(f32)
        slot = jnp.dot(
            jnp.broadcast_to(slot_ref[...].astype(f32), (8, adapters)), match, preferred_element_type=f32
        )
        rank = jnp.dot(
            jnp.broadcast_to(rank_ref[...].astype(f32), (8, adapters)), match, preferred_element_type=f32
        )
        owner = jnp.zeros((8, rows), f32)
        for s in range(1, stores):
            owner = owner + (slot >= float(s * kept)).astype(f32)
        within = slot - owner * float(kept)
        turned = owner - store.astype(f32)
        turned = jnp.where(turned < 0.0, turned + float(stores), turned)
        target = (lax.broadcasted_iota(jnp.int32, (8, rows), 0).astype(f32) == turned).astype(f32)
        earlier = (
            lax.broadcasted_iota(jnp.int32, (rows, rows), 0)
            < lax.broadcasted_iota(jnp.int32, (rows, rows), 1)
        ).astype(f32)
        before = jnp.dot(target, earlier, preferred_element_type=f32)
        place = jnp.sum(before * target, axis=0, keepdims=True) + turned[0:1] * float(capacity)
        packer_f = (
            lax.broadcasted_iota(jnp.int32, (stores * capacity, rows), 0).astype(f32) == place
        ).astype(f32)
        packer = packer_f.astype(bf16)
        packer_buf[...] = packer
        line = lax.broadcasted_iota(jnp.int32, (128, rows), 0)
        labels = jnp.where(line == 0, within[0:1] + 1.0, jnp.where(line == 1, rank[0:1], 0.0))
        labels = lax.dot_general(packer, labels.astype(bf16), NT, preferred_element_type=f32)
        label_buf[...] = labels.astype(bf16).reshape(stores, capacity, 128)

    def after_weights():
        pl.semaphore_wait(barrier, stores + column_count - 2)
        for k in range(1, stores):
            label_copy(k).start()
        for load in loads:
            load.start()

    def send_group(g):
        start = pl.multiple_of(g * span, 128)
        outgoing = jnp.dot(
            packer_buf[...], mixed_ref[:, pl.ds(start, span)], preferred_element_type=f32
        )
        outgoing = outgoing.astype(bf16)
        for k in range(stores):
            out_buf[k, g] = outgoing[k * capacity : (k + 1) * capacity]
        for k in range(1, stores):
            row_copy(k, g).start()

    attention_kernel(
        per,
        begin,
        after_weights,
        send_group,
        stream_ref,
        input_gain_ref,
        length_ref,
        query_weight_ref,
        pair_weight_ref,
        cache_ref,
        mixed_ref,
        *attention_refs,
    )
    mixed = mixed_ref[...]

    part_copies = []
    for i in range(2):
        loads[i].wait()
        part_buf[i] = jnp.dot(mixed, weight_buf[i], preferred_element_type=f32).astype(bf16)
        copy = pltpu.make_async_remote_copy(
            src_ref=part_buf.at[i],
            dst_ref=part_in.at[i],
            send_sem=part_send.at[i],
            recv_sem=part_recv.at[i],
            device_id={"tensor": partner},
            device_id_type=MESH,
        )
        copy.start()
        part_copies.append(copy)
    loads[2].wait()
    crossing = jnp.dot(mixed, weight_buf[2], preferred_element_type=f32)
    part_copies[0].wait()
    cross_buf[...] = (crossing + part_in[0].astype(f32)).astype(bf16)
    cross_copy = pltpu.make_async_remote_copy(
        src_ref=cross_buf,
        dst_ref=cross_in,
        send_sem=part_send.at[2],
        recv_sem=part_recv.at[2],
        device_id={"tensor": across},
        device_id_type=MESH,
    )
    cross_copy.start()

    for k in range(1, stores):
        label_copy(k).wait()
    label = jnp.concatenate([label_buf[0]] + [label_in[k] for k in range(stores - 1)], axis=0)
    code = label[:, 0:1].astype(f32)
    row_rank = label[:, 1:2].astype(f32)
    loads[5].wait()
    loads[6].wait()
    full = jnp.zeros((stores * capacity, kept * rank_width), f32)
    for g in range(pairs):
        for k in range(1, stores):
            row_copy(k, g).wait()
        block = jnp.concatenate([out_buf[0, g]] + [in_buf[k, g] for k in range(stores - 1)], axis=0)
        full = full + lax.dot_general(
            block, down_buf[:, g * span : (g + 1) * span], NT, preferred_element_type=f32
        )
    count = stores * capacity
    lane = lax.broadcasted_iota(jnp.int32, (count, kept * rank_width), 1).astype(f32)
    choose = jnp.logical_and(
        lane >= (code - 1.0) * float(rank_width), lane < code * float(rank_width)
    )
    full = jnp.where(choose, full, 0.0)
    coordinates = full[:, 0:128]
    for i in range(1, kept * rank_width // 128):
        coordinates = coordinates + full[:, i * 128 : (i + 1) * 128]
    low_buf[...] = coordinates.astype(bf16)
    low_copies = []
    for k in range(1, column_count):
        copy = pltpu.make_async_remote_copy(
            src_ref=low_buf,
            dst_ref=low_in.at[k - 1],
            send_sem=low_send.at[k - 1],
            recv_sem=low_recv.at[k - 1],
            device_id={"tensor": (column + k) % column_count},
            device_id_type=MESH,
        )
        copy.start()
        low_copies.append(copy)

    loads[3].wait()
    own = jnp.dot(mixed, weight_buf[3], preferred_element_type=f32)
    part_copies[1].wait()
    own = own + part_in[1].astype(f32)

    for k in range(column_count - 1):
        low_copies[k].wait()
        coordinates = coordinates + low_in[k].astype(f32)
    place_in_rank = lax.broadcasted_iota(jnp.int32, (count, 128), 1) % rank_width
    live = place_in_rank.astype(f32) < row_rank
    narrow = jnp.where(live, coordinates * (adapter_strength / jnp.maximum(row_rank, 1.0)), 0.0)
    spread = jnp.concatenate([narrow] * (kept * rank_width // 128), axis=1)
    spread = jnp.where(choose, spread, 0.0).astype(bf16)
    wide = jnp.dot(spread, up_buf[...], preferred_element_type=f32).astype(bf16)
    back_buf[...] = wide.reshape(stores, capacity, portion)
    back_copies = []
    for k in range(1, stores):
        copy = pltpu.make_async_remote_copy(
            src_ref=back_buf.at[k],
            dst_ref=back_in.at[k - 1],
            send_sem=back_send.at[k - 1],
            recv_sem=back_recv.at[k - 1],
            device_id={"store": (store + stores - k) % stores},
            device_id_type=MESH,
        )
        copy.start()
        back_copies.append(copy)

    unpacker = packer_buf[...].astype(f32).T.astype(bf16)
    cross_copy.wait()
    own = own + cross_in[...].astype(f32)
    for copy in back_copies:
        copy.wait()
    returned = jnp.concatenate([back_buf[0]] + [back_in[k] for k in range(stores - 1)], axis=0)
    projected = own + jnp.dot(unpacker, returned, preferred_element_type=f32)

    squares = jnp.sum(projected * projected, axis=1, keepdims=True)
    stat_buf[...] = jnp.broadcast_to(squares, (rows, 128)).T[0:8]
    stat_copies = []
    for k in range(1, column_count):
        copy = pltpu.make_async_remote_copy(
            src_ref=stat_buf,
            dst_ref=stat_in.at[k - 1],
            send_sem=stat_send.at[k - 1],
            recv_sem=stat_recv.at[k - 1],
            device_id={"tensor": (column + k) % column_count},
            device_id_type=MESH,
        )
        copy.start()
        stat_copies.append(copy)
    loads[4].wait()
    total = stat_buf[0:1]
    for k in range(column_count - 1):
        stat_copies[k].wait()
        total = total + stat_in[k, 0:1]
    total = jnp.broadcast_to(total, (128, rows)).T[:, 0:1]
    factor = lax.rsqrt(total * (1.0 / width) + epsilon)
    out_ref[...] = (
        stream_buf[...].astype(f32) + projected * factor * gain_ref[...].astype(f32)
    ).astype(bf16)


def exchange(
    stream,
    input_gain,
    lengths,
    query_weight,
    pair_weight,
    cache,
    index,
    slots,
    ranks,
    down,
    up,
    gain,
    weight,
):
    stores = lax.axis_size("store")
    column_count = lax.axis_size("tensor")
    rows, width = stream.shape
    depth = query_weight.shape[1]
    per = depth // pair_weight.shape[2]
    pairs = pair_weight.shape[2] // HEAD_WIDTH
    span = depth // pairs
    own_scratch = attention_scratch(rows, width, query_weight, pair_weight, cache)
    kept = down.shape[1]
    rank_width = down.shape[2]
    portion = up.shape[2]
    capacity = rows // 4
    down = jnp.transpose(down, (1, 2, 0)).reshape(kept * rank_width, depth)
    up = up.reshape(kept * rank_width, portion)
    bf16 = jnp.bfloat16
    dma = pltpu.SemaphoreType.DMA
    vmem = pl.BlockSpec(memory_space=pltpu.VMEM)
    hbm = pl.BlockSpec(memory_space=pl.ANY)
    return pl.pallas_call(
        functools.partial(
            exchange_kernel, stores, column_count, kept, capacity, per
        ),
        out_shape=jax.ShapeDtypeStruct((rows, portion), bf16),
        in_specs=[vmem] * 6 + [hbm] * 7,
        out_specs=vmem,
        scratch_shapes=[
            pltpu.VMEM((rows, depth), bf16),
            pltpu.VMEM((kept * rank_width, depth), bf16),
            pltpu.VMEM((kept * rank_width, portion), bf16),
            pltpu.VMEM((stores * capacity, rows), bf16),
            pltpu.VMEM((column_count, depth, portion), bf16),
            pltpu.VMEM((rows, portion), bf16),
            pltpu.VMEM((stores, pairs, capacity, span), bf16),
            pltpu.VMEM((stores - 1, pairs, capacity, span), bf16),
            pltpu.VMEM((stores, capacity, 128), bf16),
            pltpu.VMEM((stores - 1, capacity, 128), bf16),
            pltpu.VMEM((2, rows, portion), bf16),
            pltpu.VMEM((2, rows, portion), bf16),
            pltpu.VMEM((rows, portion), bf16),
            pltpu.VMEM((rows, portion), bf16),
            pltpu.VMEM((stores * capacity, 128), bf16),
            pltpu.VMEM((column_count - 1, stores * capacity, 128), bf16),
            pltpu.VMEM((stores, capacity, portion), bf16),
            pltpu.VMEM((stores - 1, capacity, portion), bf16),
            pltpu.VMEM((8, rows), jnp.float32),
            pltpu.VMEM((column_count - 1, 8, rows), jnp.float32),
            dma((column_count + 3,)),
            dma((stores - 1, pairs)),
            dma((stores - 1, pairs)),
            dma((stores - 1,)),
            dma((stores - 1,)),
            dma((3,)),
            dma((3,)),
            dma((column_count - 1,)),
            dma((column_count - 1,)),
            dma((stores - 1,)),
            dma((stores - 1,)),
            dma((column_count - 1,)),
            dma((column_count - 1,)),
        ]
        + own_scratch,
        compiler_params=pltpu.CompilerParams(
            collective_id=0, has_side_effects=True, vmem_limit_bytes=62 << 20
        ),
    )(
        input_gain.reshape(1, -1),
        lengths.reshape(1, -1),
        index.reshape(1, -1),
        slots.reshape(1, -1),
        ranks.reshape(1, -1),
        gain.reshape(1, -1),
        stream,
        query_weight,
        pair_weight,
        cache,
        down,
        up,
        weight,
    )


def per_device(
    stream,
    input_norm_gain,
    output_norm_gain,
    query_projection,
    key_value_weight,
    output_projection,
    cached_key_value,
    row_cache_length,
    row_adapter_index,
    adapter_slot_table,
    adapter_rank_table,
    adapter_down_weight,
    adapter_up_weight,
):
    stores = lax.axis_size("store")
    column = lax.axis_index("tensor")
    row_count, width = stream.shape
    kept_factors = adapter_down_weight.shape[1]
    rank_padding = adapter_down_weight.shape[2]
    adapter_portion = adapter_up_weight.shape[2]
    capacity = row_count // 4
    if lax.axis_size("tensor") == 4 and adapter_portion % 128 == 0 and row_count == 128:
        return exchange(
            stream,
            input_norm_gain,
            row_cache_length,
            query_projection,
            key_value_weight,
            cached_key_value,
            row_adapter_index,
            adapter_slot_table,
            adapter_rank_table,
            adapter_down_weight,
            adapter_up_weight,
            output_norm_gain,
            output_projection,
        )
    mixed = attention(
        stream,
        input_norm_gain,
        row_cache_length,
        query_projection,
        key_value_weight,
        cached_key_value,
    )
    stream_f = stream.astype(jnp.float32)
    adapters = adapter_slot_table.shape[0]
    match = row_adapter_index[:, None] == jnp.arange(adapters)[None, :]
    slot = jnp.sum(jnp.where(match, adapter_slot_table[None, :], 0), axis=1)
    adapter_rank_value = jnp.sum(jnp.where(match, adapter_rank_table[None, :], 0), axis=1)
    owner = slot // kept_factors
    within = slot - owner * kept_factors
    target = (owner[:, None] == jnp.arange(stores)[None, :]).astype(jnp.int32)
    before = jnp.cumsum(target, axis=0) - target
    bucket = owner * capacity + jnp.sum(before * target, axis=1)
    packer = (bucket[None, :] == jnp.arange(stores * capacity)[:, None]).astype(jnp.bfloat16)
    outgoing = jnp.dot(packer, mixed, preferred_element_type=jnp.float32).astype(jnp.bfloat16)
    outgoing = outgoing.reshape(stores, capacity, -1)
    labels = jnp.stack(
        [(within + 1).astype(jnp.float32), adapter_rank_value.astype(jnp.float32)], axis=-1
    )
    labels = (
        jnp.dot(packer.astype(jnp.float32), labels)
        .astype(jnp.bfloat16)
        .reshape(stores, capacity, 2)
    )
    down_factor = adapter_down_weight.reshape(
        adapter_down_weight.shape[0], kept_factors * rank_padding
    )
    up_factor = adapter_up_weight.reshape(kept_factors * rank_padding, adapter_portion)
    block = lax.all_to_all(outgoing, "store", split_axis=0, concat_axis=0, tiled=True)
    marks = lax.all_to_all(labels, "store", split_axis=0, concat_axis=0, tiled=True)
    count = block.shape[0] * block.shape[1]
    flat = block.reshape(count, -1)
    code = marks[..., 0].reshape(count).astype(jnp.float32)
    row_rank_value = marks[..., 1].reshape(count).astype(jnp.float32)
    choose = code[:, None] - 1.0 == jnp.arange(kept_factors, dtype=jnp.float32)[None, :]
    gather_places = jnp.dot(flat, down_factor, preferred_element_type=jnp.float32).reshape(
        count, kept_factors, rank_padding
    )
    gather_places = jnp.sum(gather_places * choose.astype(jnp.float32)[:, :, None], axis=1)
    gather_places = lax.psum(gather_places, "tensor")
    live_positions = (
        jnp.arange(rank_padding, dtype=jnp.float32)[None, :] < row_rank_value[:, None]
    ).astype(jnp.float32)
    narrow_input = (
        gather_places
        * live_positions
        * (adapter_strength / jnp.maximum(row_rank_value, 1.0))[:, None]
    ).astype(jnp.bfloat16)
    rank_spread = (narrow_input[:, None, :] * choose.astype(jnp.bfloat16)[:, :, None]).reshape(
        count, kept_factors * rank_padding
    )
    narrow_output = jnp.dot(rank_spread, up_factor, preferred_element_type=jnp.float32).astype(
        jnp.bfloat16
    )
    narrow_output = narrow_output.reshape(block.shape[0], block.shape[1], adapter_portion)
    returned = lax.all_to_all(narrow_output, "store", split_axis=0, concat_axis=0, tiled=True)
    low_home = lax.dot_general(
        packer,
        returned.reshape(stores * capacity, adapter_portion),
        (((0,), (0,)), ((), ())),
        preferred_element_type=jnp.float32,
    )
    partial_sum = jnp.dot(mixed, output_projection, preferred_element_type=jnp.float32)
    gain = output_norm_gain.astype(jnp.float32)
    stream_mine = lax.dynamic_slice_in_dim(stream_f, column * adapter_portion, adapter_portion, 1)
    piece = (
        lax.dynamic_slice_in_dim(partial_sum, column * adapter_portion, adapter_portion, 1)
        + low_home
    )
    summand = lax.dynamic_update_slice_in_dim(partial_sum, piece, column * adapter_portion, 1)
    projected = lax.psum(summand, "tensor")
    mean = jnp.mean(projected * projected, axis=-1, keepdims=True)
    mine = lax.dynamic_slice_in_dim(projected, column * adapter_portion, adapter_portion, 1)
    return (stream_mine + mine * lax.rsqrt(mean + epsilon) * gain).astype(jnp.bfloat16)


def solution(mesh):
    in_specs = (
        P(("groups", "store"), None),
        P(),
        P("tensor"),
        P(None, "tensor"),
        P(None, None, "tensor"),
        P("tensor", None),
        P(None, ("groups", "store"), "tensor", None, None),
        P(("groups", "store")),
        P(("groups", "store")),
        P("groups"),
        P("groups"),
        P("tensor", ("groups", "store"), None),
        P(("groups", "store"), None, "tensor"),
    )
    out_specs = P(("groups", "store"), "tensor")
    return jax.shard_map(
        per_device, mesh=mesh, in_specs=in_specs, out_specs=out_specs, check_vma=False
    )
```

```python
import functools
import math

import jax
import jax.numpy as jnp
from jax import lax
from jax.experimental import pallas as pl
from jax.experimental.pallas import tpu as pltpu
from jax.sharding import PartitionSpec as P

MESH = pl.DeviceIdType.MESH
NT = (((1,), (1,)), ((), ()))

HEAD_WIDTH = 128


epsilon = 1e-06
adapter_strength = 32.0
query_factor = 144.0 ** (-0.5)
rope_base = 10000.0


def attention_kernel(
    per,
    begin,
    after_weights,
    after_group,
    stream_ref,
    gain_ref,
    length_ref,
    query_weight_ref,
    pair_weight_ref,
    cache_ref,
    out_ref,
    stream_buf,
    normed_buf,
    query_buf,
    pair_buf,
    cache_buf,
    query_sum,
    pair_sum,
    query_heads,
    key_heads,
    value_heads,
    length_buf,
    query_sem,
    pair_sem,
    cache_sem,
    stream_sem,
):
    rows, width = stream_buf.shape
    slots = cache_buf.shape[1]
    chunks, step, _ = query_buf.shape
    pairs = key_heads.shape[0]
    group = 128 // per
    blocks = rows // group
    parts = pairs * blocks
    octets = group // 8
    f32 = jnp.float32
    bf16 = jnp.bfloat16

    def query_copy(c):
        return pltpu.make_async_copy(
            query_weight_ref.at[pl.ds(c * step, step)], query_buf.at[c], query_sem.at[c]
        )

    def pair_copy(c):
        return pltpu.make_async_copy(
            pair_weight_ref.at[pl.ds(c * step, step)], pair_buf.at[c], pair_sem.at[c]
        )

    def cache_copy(kind, part):
        start = pl.multiple_of((part % blocks) * group, 8)
        return pltpu.make_async_copy(
            cache_ref.at[kind, pl.ds(start, group), part // blocks],
            cache_buf.at[kind, part % slots],
            cache_sem.at[kind, part % slots],
        )

    stream_copy = pltpu.make_async_copy(stream_ref, stream_buf, stream_sem)
    stream_copy.start()
    for c in range(chunks):
        pair_copy(c).start()
        query_copy(c).start(priority=1)
    if begin is not None:
        begin()
    stream_copy.wait()
    stream = stream_buf[...].astype(f32)
    scale = lax.rsqrt(jnp.mean(stream * stream, axis=-1, keepdims=True) + epsilon)
    gain = gain_ref[...].astype(f32).reshape(1, width)
    for c in range(chunks):
        cut = slice(c * step, (c + 1) * step)
        normed_buf[c] = (stream[:, cut] * scale * gain[:, cut]).astype(bf16)
    length = jnp.broadcast_to(length_ref[...].astype(f32), (128, rows)).T
    length_buf[...] = length
    lane = lax.broadcasted_iota(jnp.int32, (rows, 128), 1)
    exponent = (lane % 64).astype(f32) * (-2.0 * math.log(rope_base) / HEAD_WIDTH)
    angle = length * jnp.exp(exponent)
    cosine = jnp.cos(angle)
    sine = jnp.where(lane < 64, -jnp.sin(angle), jnp.sin(angle))

    near = lax.broadcasted_iota(jnp.int32, (128, 512), 0)
    far = lax.broadcasted_iota(jnp.int32, (128, 512), 1)
    spreader = (
        jnp.where(far < 256, near * 2, near * 2 + 257) == far
    ).astype(f32).astype(bf16)
    query_sum[...] = jnp.zeros_like(query_sum)
    pair_sum[...] = jnp.zeros_like(pair_sum)

    def project(c, carry):
        normed = normed_buf[c]
        wide = [
            jnp.dot(
                normed[:, i * 128 : (i + 1) * 128], spreader, preferred_element_type=f32
            ).astype(bf16)
            for i in range(step // 128)
        ]
        both = jnp.concatenate(
            [
                jnp.concatenate([w[:, :256] for w in wide], axis=1),
                jnp.concatenate([w[:, 256:] for w in wide], axis=1),
            ],
            axis=0,
        )
        pair_copy(c).wait()
        weight = pair_buf[c].reshape(2 * step, pair_buf.shape[3])
        pair_sum[...] += jnp.dot(both, weight, preferred_element_type=f32)
        query_copy(c).wait()
        query_sum[...] += jnp.dot(normed, query_buf[c], preferred_element_type=f32)

        @pl.when(c < slots)
        def _():
            cache_copy(0, c).start()
            cache_copy(1, c).start(priority=1)

        return carry

    lax.fori_loop(0, chunks, project, 0)
    if after_weights is not None:
        after_weights()

    def turned(values):
        return values * cosine + pltpu.roll(values, 64, 1) * sine

    for h in range(pairs * per):
        query_heads[h] = turned(query_sum[:, h * 128 : (h + 1) * 128]).astype(bf16)
    for g in range(pairs):
        cut = slice(g * 128, (g + 1) * 128)
        key_heads[g] = turned(pair_sum[0:rows, cut]).astype(bf16)
        value_heads[g] = pair_sum[rows : 2 * rows, cut].astype(bf16)

    def stacked(pieces):
        return jnp.stack([p.reshape(octets, 8, 128) for p in pieces], axis=1).reshape(128, 128)

    def attend_part(part, carry):
        g = part // blocks
        start = pl.multiple_of((part % blocks) * group, 8)
        here = pl.ds(start, group)
        query = stacked([query_heads[g * per + i, here].astype(f32) for i in range(per)])
        key_new = stacked([key_heads[g, here].astype(f32)] * per)
        value_new = stacked([value_heads[g, here].astype(f32)] * per)
        limit = stacked([length_buf[here]] * per)
        own = jnp.sum(query * key_new, axis=1, keepdims=True) * query_factor
        query = query.astype(bf16)
        across = lax.broadcasted_iota(jnp.int32, (128, 128), 1)
        row_of_lane = (across // (8 * per)) * 8 + across % 8
        scores = jnp.zeros((128, 128), f32)
        slot = part % slots
        cache_copy(0, part).wait()
        for j in range(octets):
            keys = cache_buf[0, slot, 8 * j : 8 * j + 8].reshape(1024, 128)
            product = lax.dot_general(keys, query, NT, preferred_element_type=f32)
            for r in range(8):
                scores = jnp.where(
                    row_of_lane == 8 * j + r, product[128 * r : 128 * (r + 1)], scores
                )
        scores = scores.T * query_factor
        scores = jnp.where(across.astype(f32) < limit, scores, -jnp.inf)
        top = jnp.maximum(jnp.max(scores, axis=1, keepdims=True), own)
        weights = jnp.exp(scores - top)
        own_weight = jnp.exp(own - top)
        total = jnp.sum(weights, axis=1, keepdims=True) + own_weight
        probs = weights / total
        own_prob = (own_weight / total).astype(bf16).astype(f32)
        tall = 8 * per
        row_in_octet = lax.broadcasted_iota(jnp.int32, (tall, 128), 0) % 8
        mixed = []
        cache_copy(1, part).wait()
        for j in range(octets):
            piece = probs[tall * j : tall * (j + 1)]
            spread = jnp.concatenate(
                [jnp.where(row_in_octet == r, piece, 0.0).astype(bf16) for r in range(8)], axis=1
            )
            values = cache_buf[1, slot, 8 * j : 8 * j + 8].reshape(1024, 128)
            mixed.append(jnp.dot(spread, values, preferred_element_type=f32))
        mixed = jnp.concatenate(mixed, axis=0) + own_prob * value_new
        mixed = mixed.astype(bf16).astype(f32).reshape(octets, per, 8, 128)
        for i in range(per):
            column = pl.multiple_of((g * per + i) * 128, 128)
            out_ref[here, pl.ds(column, 128)] = mixed[:, i].reshape(group, 128).astype(bf16)

        @pl.when(part + slots < parts)
        def _():
            cache_copy(0, part + slots).start()
            cache_copy(1, part + slots).start(priority=1)

        if after_group is not None:

            @pl.when(part % blocks == blocks - 1)
            def _():
                after_group(g)

        return carry

    lax.fori_loop(0, parts, attend_part, 0)


def attention_scratch(rows, width, query_weight, pair_weight, cache):
    step = 512
    chunks = width // step
    pairs = pair_weight.shape[2] // HEAD_WIDTH
    heads = query_weight.shape[1] // HEAD_WIDTH
    group = 128 * pairs // heads
    slots = min(pairs * (rows // group), 5)
    bf16 = jnp.bfloat16
    dma = pltpu.SemaphoreType.DMA
    return [
        pltpu.VMEM((rows, width), bf16),
        pltpu.VMEM((chunks, rows, step), bf16),
        pltpu.VMEM((chunks, step, heads * HEAD_WIDTH), bf16),
        pltpu.VMEM((chunks, step, 2, pairs * HEAD_WIDTH), bf16),
        pltpu.VMEM((2, slots, group, cache.shape[3], HEAD_WIDTH), bf16),
        pltpu.VMEM((rows, heads * HEAD_WIDTH), jnp.float32),
        pltpu.VMEM((2 * rows, pairs * HEAD_WIDTH), jnp.float32),
        pltpu.VMEM((heads, rows, HEAD_WIDTH), bf16),
        pltpu.VMEM((pairs, rows, HEAD_WIDTH), bf16),
        pltpu.VMEM((pairs, rows, HEAD_WIDTH), bf16),
        pltpu.VMEM((rows, HEAD_WIDTH), jnp.float32),
        dma((chunks,)),
        dma((chunks,)),
        dma((2, slots)),
        dma,
    ]


def attention(stream, gain, lengths, query_weight, pair_weight, cache):
    rows, width = stream.shape
    heads = query_weight.shape[1] // HEAD_WIDTH
    per = query_weight.shape[1] // pair_weight.shape[2]
    vmem = pl.BlockSpec(memory_space=pltpu.VMEM)
    hbm = pl.BlockSpec(memory_space=pl.ANY)
    return pl.pallas_call(
        functools.partial(attention_kernel, per, None, None, None),
        out_shape=jax.ShapeDtypeStruct((rows, heads * HEAD_WIDTH), jnp.bfloat16),
        in_specs=[hbm] + [vmem] * 2 + [hbm] * 3,
        out_specs=vmem,
        scratch_shapes=attention_scratch(rows, width, query_weight, pair_weight, cache),
        compiler_params=pltpu.CompilerParams(vmem_limit_bytes=60 << 20),
    )(stream, gain, lengths.reshape(1, -1), query_weight, pair_weight, cache)


def exchange_kernel(
    stores,
    column_count,
    kept,
    capacity,
    per,
    input_gain_ref,
    length_ref,
    index_ref,
    slot_ref,
    rank_ref,
    gain_ref,
    stream_ref,
    query_weight_ref,
    pair_weight_ref,
    cache_ref,
    down_ref,
    up_ref,
    weight_ref,
    out_ref,
    mixed_ref,
    down_buf,
    up_buf,
    packer_buf,
    weight_buf,
    stream_buf,
    out_buf,
    in_buf,
    label_buf,
    label_in,
    part_buf,
    part_in,
    cross_buf,
    cross_in,
    low_buf,
    low_in,
    back_buf,
    back_in,
    stat_buf,
    stat_in,
    load_sem,
    row_send,
    row_recv,
    label_send,
    label_recv,
    part_send,
    part_recv,
    low_send,
    low_recv,
    back_send,
    back_recv,
    stat_send,
    stat_recv,
    *attention_refs,
):
    rows, depth = mixed_ref.shape
    portion = gain_ref.shape[0]
    rank_width = down_ref.shape[0] // kept
    pairs = out_buf.shape[1]
    span = depth // pairs
    width = portion * column_count
    f32 = jnp.float32
    bf16 = jnp.bfloat16
    store = lax.axis_index("store")
    column = lax.axis_index("tensor")
    chip = column // 2
    core = column % 2
    chunks = [(1 - chip) * 2 + 1 - core, chip * 2 + 1 - core, (1 - chip) * 2 + core, column]
    partner = chip * 2 + 1 - core
    across = (1 - chip) * 2 + core

    loads = []
    for i, chunk in enumerate(chunks):
        start = pl.multiple_of(chunk * portion, 128)
        loads.append(
            pltpu.make_async_copy(
                weight_ref.at[:, pl.ds(start, portion)], weight_buf.at[i], load_sem.at[i]
            )
        )
    mine = pl.multiple_of(column * portion, 128)
    loads.append(
        pltpu.make_async_copy(
            stream_ref.at[:, pl.ds(mine, portion)], stream_buf, load_sem.at[column_count]
        )
    )
    loads.append(pltpu.make_async_copy(down_ref, down_buf, load_sem.at[column_count + 1]))
    loads.append(pltpu.make_async_copy(up_ref, up_buf, load_sem.at[column_count + 2]))

    def label_copy(k):
        return pltpu.make_async_remote_copy(
            src_ref=label_buf.at[k],
            dst_ref=label_in.at[k - 1],
            send_sem=label_send.at[k - 1],
            recv_sem=label_recv.at[k - 1],
            device_id={"store": (store + k) % stores},
            device_id_type=MESH,
        )

    def row_copy(k, g):
        return pltpu.make_async_remote_copy(
            src_ref=out_buf.at[k, g],
            dst_ref=in_buf.at[k - 1, g],
            send_sem=row_send.at[k - 1, g],
            recv_sem=row_recv.at[k - 1, g],
            device_id={"store": (store + k) % stores},
            device_id_type=MESH,
        )

    barrier = pltpu.get_barrier_semaphore()

    def begin():
        for k in range(1, stores):
            pl.semaphore_signal(
                barrier, inc=1, device_id={"store": (store + k) % stores}, device_id_type=MESH
            )
        for k in range(1, column_count):
            pl.semaphore_signal(
                barrier, inc=1, device_id={"tensor": (column + k) % column_count}, device_id_type=MESH
            )

        adapters = slot_ref.shape[1]
        match = (
            lax.broadcasted_iota(jnp.int32, (adapters, rows), 0) == index_ref[...]
        ).astype(f32)
        slot = jnp.dot(
            jnp.broadcast_to(slot_ref[...].astype(f32), (8, adapters)), match, preferred_element_type=f32
        )
        rank = jnp.dot(
            jnp.broadcast_to(rank_ref[...].astype(f32), (8, adapters)), match, preferred_element_type=f32
        )
        owner = jnp.zeros((8, rows), f32)
        for s in range(1, stores):
            owner = owner + (slot >= float(s * kept)).astype(f32)
        within = slot - owner * float(kept)
        turned = owner - store.astype(f32)
        turned = jnp.where(turned < 0.0, turned + float(stores), turned)
        target = (lax.broadcasted_iota(jnp.int32, (8, rows), 0).astype(f32) == turned).astype(f32)
        earlier = (
            lax.broadcasted_iota(jnp.int32, (rows, rows), 0)
            < lax.broadcasted_iota(jnp.int32, (rows, rows), 1)
        ).astype(f32)
        before = jnp.dot(target, earlier, preferred_element_type=f32)
        place = jnp.sum(before * target, axis=0, keepdims=True) + turned[0:1] * float(capacity)
        packer_f = (
            lax.broadcasted_iota(jnp.int32, (stores * capacity, rows), 0).astype(f32) == place
        ).astype(f32)
        packer = packer_f.astype(bf16)
        packer_buf[...] = packer
        line = lax.broadcasted_iota(jnp.int32, (128, rows), 0)
        labels = jnp.where(line == 0, within[0:1] + 1.0, jnp.where(line == 1, rank[0:1], 0.0))
        labels = lax.dot_general(packer, labels.astype(bf16), NT, preferred_element_type=f32)
        label_buf[...] = labels.astype(bf16).reshape(stores, capacity, 128)

    def after_weights():
        pl.semaphore_wait(barrier, stores + column_count - 2)
        for k in range(1, stores):
            label_copy(k).start()
        for i, load in enumerate(loads):
            load.start(priority=i % 2)

    def send_group(g):
        start = pl.multiple_of(g * span, 128)
        outgoing = jnp.dot(
            packer_buf[...], mixed_ref[:, pl.ds(start, span)], preferred_element_type=f32
        )
        outgoing = outgoing.astype(bf16)
        for k in range(stores):
            out_buf[k, g] = outgoing[k * capacity : (k + 1) * capacity]
        for k in range(1, stores):
            row_copy(k, g).start()

    attention_kernel(
        per,
        begin,
        after_weights,
        send_group,
        stream_ref,
        input_gain_ref,
        length_ref,
        query_weight_ref,
        pair_weight_ref,
        cache_ref,
        mixed_ref,
        *attention_refs,
    )
    mixed = mixed_ref[...]

    part_copies = []
    for i in range(2):
        loads[i].wait()
        part_buf[i] = jnp.dot(mixed, weight_buf[i], preferred_element_type=f32).astype(bf16)
        copy = pltpu.make_async_remote_copy(
            src_ref=part_buf.at[i],
            dst_ref=part_in.at[i],
            send_sem=part_send.at[i],
            recv_sem=part_recv.at[i],
            device_id={"tensor": partner},
            device_id_type=MESH,
        )
        copy.start()
        part_copies.append(copy)
    for k in range(1, stores):
        label_copy(k).wait()
    label = jnp.concatenate([label_buf[0]] + [label_in[k] for k in range(stores - 1)], axis=0)
    code = label[:, 0:1].astype(f32)
    row_rank = label[:, 1:2].astype(f32)
    loads[5].wait()
    loads[6].wait()
    full = jnp.zeros((stores * capacity, kept * rank_width), f32)
    for g in range(pairs):
        for k in range(1, stores):
            row_copy(k, g).wait()
        block = jnp.concatenate([out_buf[0, g]] + [in_buf[k, g] for k in range(stores - 1)], axis=0)
        full = full + lax.dot_general(
            block, down_buf[:, g * span : (g + 1) * span], NT, preferred_element_type=f32
        )
    count = stores * capacity
    lane = lax.broadcasted_iota(jnp.int32, (count, kept * rank_width), 1).astype(f32)
    choose = jnp.logical_and(
        lane >= (code - 1.0) * float(rank_width), lane < code * float(rank_width)
    )
    full = jnp.where(choose, full, 0.0)
    coordinates = full[:, 0:128]
    for i in range(1, kept * rank_width // 128):
        coordinates = coordinates + full[:, i * 128 : (i + 1) * 128]
    low_buf[...] = coordinates.astype(bf16)
    low_copies = []
    for k in range(1, column_count):
        copy = pltpu.make_async_remote_copy(
            src_ref=low_buf,
            dst_ref=low_in.at[k - 1],
            send_sem=low_send.at[k - 1],
            recv_sem=low_recv.at[k - 1],
            device_id={"tensor": (column + k) % column_count},
            device_id_type=MESH,
        )
        copy.start()
        low_copies.append(copy)

    loads[2].wait()
    crossing = jnp.dot(mixed, weight_buf[2], preferred_element_type=f32)
    part_copies[0].wait()
    cross_buf[...] = (crossing + part_in[0].astype(f32)).astype(bf16)
    cross_copy = pltpu.make_async_remote_copy(
        src_ref=cross_buf,
        dst_ref=cross_in,
        send_sem=part_send.at[2],
        recv_sem=part_recv.at[2],
        device_id={"tensor": across},
        device_id_type=MESH,
    )
    cross_copy.start()

    loads[3].wait()
    own = jnp.dot(mixed, weight_buf[3], preferred_element_type=f32)
    part_copies[1].wait()
    own = own + part_in[1].astype(f32)

    for k in range(column_count - 1):
        low_copies[k].wait()
        coordinates = coordinates + low_in[k].astype(f32)
    place_in_rank = lax.broadcasted_iota(jnp.int32, (count, 128), 1) % rank_width
    live = place_in_rank.astype(f32) < row_rank
    narrow = jnp.where(live, coordinates * (adapter_strength / jnp.maximum(row_rank, 1.0)), 0.0)
    spread = jnp.concatenate([narrow] * (kept * rank_width // 128), axis=1)
    spread = jnp.where(choose, spread, 0.0).astype(bf16)
    wide = jnp.dot(spread, up_buf[...], preferred_element_type=f32).astype(bf16)
    back_buf[...] = wide.reshape(stores, capacity, portion)
    back_copies = []
    for k in range(1, stores):
        copy = pltpu.make_async_remote_copy(
            src_ref=back_buf.at[k],
            dst_ref=back_in.at[k - 1],
            send_sem=back_send.at[k - 1],
            recv_sem=back_recv.at[k - 1],
            device_id={"store": (store + stores - k) % stores},
            device_id_type=MESH,
        )
        copy.start()
        back_copies.append(copy)

    unpacker = packer_buf[...].astype(f32).T.astype(bf16)
    cross_copy.wait()
    own = own + cross_in[...].astype(f32)
    for copy in back_copies:
        copy.wait()
    returned = jnp.concatenate([back_buf[0]] + [back_in[k] for k in range(stores - 1)], axis=0)
    projected = own + jnp.dot(unpacker, returned, preferred_element_type=f32)

    squares = jnp.sum(projected * projected, axis=1, keepdims=True)
    stat_buf[...] = jnp.broadcast_to(squares, (rows, 128)).T[0:8]
    stat_copies = []
    for k in range(1, column_count):
        copy = pltpu.make_async_remote_copy(
            src_ref=stat_buf,
            dst_ref=stat_in.at[k - 1],
            send_sem=stat_send.at[k - 1],
            recv_sem=stat_recv.at[k - 1],
            device_id={"tensor": (column + k) % column_count},
            device_id_type=MESH,
        )
        copy.start()
        stat_copies.append(copy)
    loads[4].wait()
    total = stat_buf[0:1]
    for k in range(column_count - 1):
        stat_copies[k].wait()
        total = total + stat_in[k, 0:1]
    total = jnp.broadcast_to(total, (128, rows)).T[:, 0:1]
    factor = lax.rsqrt(total * (1.0 / width) + epsilon)
    out_ref[...] = (
        stream_buf[...].astype(f32)
        + projected * factor * gain_ref[...].astype(f32).reshape(1, portion)
    ).astype(bf16)


def exchange(
    stream,
    input_gain,
    lengths,
    query_weight,
    pair_weight,
    cache,
    index,
    slots,
    ranks,
    down,
    up,
    gain,
    weight,
):
    stores = lax.axis_size("store")
    column_count = lax.axis_size("tensor")
    rows, width = stream.shape
    depth = query_weight.shape[1]
    per = depth // pair_weight.shape[2]
    pairs = pair_weight.shape[2] // HEAD_WIDTH
    span = depth // pairs
    own_scratch = attention_scratch(rows, width, query_weight, pair_weight, cache)
    kept = down.shape[1]
    rank_width = down.shape[2]
    portion = up.shape[2]
    capacity = rows // 4
    down = jnp.transpose(down, (1, 2, 0)).reshape(kept * rank_width, depth)
    up = up.reshape(kept * rank_width, portion)
    bf16 = jnp.bfloat16
    dma = pltpu.SemaphoreType.DMA
    vmem = pl.BlockSpec(memory_space=pltpu.VMEM)
    hbm = pl.BlockSpec(memory_space=pl.ANY)
    return pl.pallas_call(
        functools.partial(
            exchange_kernel, stores, column_count, kept, capacity, per
        ),
        out_shape=jax.ShapeDtypeStruct((rows, portion), bf16),
        in_specs=[vmem] * 6 + [hbm] * 7,
        out_specs=vmem,
        scratch_shapes=[
            pltpu.VMEM((rows, depth), bf16),
            pltpu.VMEM((kept * rank_width, depth), bf16),
            pltpu.VMEM((kept * rank_width, portion), bf16),
            pltpu.VMEM((stores * capacity, rows), bf16),
            pltpu.VMEM((column_count, depth, portion), bf16),
            pltpu.VMEM((rows, portion), bf16),
            pltpu.VMEM((stores, pairs, capacity, span), bf16),
            pltpu.VMEM((stores - 1, pairs, capacity, span), bf16),
            pltpu.VMEM((stores, capacity, 128), bf16),
            pltpu.VMEM((stores - 1, capacity, 128), bf16),
            pltpu.VMEM((2, rows, portion), bf16),
            pltpu.VMEM((2, rows, portion), bf16),
            pltpu.VMEM((rows, portion), bf16),
            pltpu.VMEM((rows, portion), bf16),
            pltpu.VMEM((stores * capacity, 128), bf16),
            pltpu.VMEM((column_count - 1, stores * capacity, 128), bf16),
            pltpu.VMEM((stores, capacity, portion), bf16),
            pltpu.VMEM((stores - 1, capacity, portion), bf16),
            pltpu.VMEM((8, rows), jnp.float32),
            pltpu.VMEM((column_count - 1, 8, rows), jnp.float32),
            dma((column_count + 3,)),
            dma((stores - 1, pairs)),
            dma((stores - 1, pairs)),
            dma((stores - 1,)),
            dma((stores - 1,)),
            dma((3,)),
            dma((3,)),
            dma((column_count - 1,)),
            dma((column_count - 1,)),
            dma((stores - 1,)),
            dma((stores - 1,)),
            dma((column_count - 1,)),
            dma((column_count - 1,)),
        ]
        + own_scratch,
        compiler_params=pltpu.CompilerParams(
            collective_id=0, has_side_effects=True, vmem_limit_bytes=62 << 20
        ),
    )(
        input_gain,
        lengths.reshape(1, -1),
        index.reshape(1, -1),
        slots.reshape(1, -1),
        ranks.reshape(1, -1),
        gain,
        stream,
        query_weight,
        pair_weight,
        cache,
        down,
        up,
        weight,
    )


def per_device(
    stream,
    input_norm_gain,
    output_norm_gain,
    query_projection,
    key_value_weight,
    output_projection,
    cached_key_value,
    row_cache_length,
    row_adapter_index,
    adapter_slot_table,
    adapter_rank_table,
    adapter_down_weight,
    adapter_up_weight,
):
    stores = lax.axis_size("store")
    column = lax.axis_index("tensor")
    row_count, width = stream.shape
    kept_factors = adapter_down_weight.shape[1]
    rank_padding = adapter_down_weight.shape[2]
    adapter_portion = adapter_up_weight.shape[2]
    capacity = row_count // 4
    if lax.axis_size("tensor") == 4 and adapter_portion % 128 == 0 and row_count == 128:
        return exchange(
            stream,
            input_norm_gain,
            row_cache_length,
            query_projection,
            key_value_weight,
            cached_key_value,
            row_adapter_index,
            adapter_slot_table,
            adapter_rank_table,
            adapter_down_weight,
            adapter_up_weight,
            output_norm_gain,
            output_projection,
        )
    mixed = attention(
        stream,
        input_norm_gain,
        row_cache_length,
        query_projection,
        key_value_weight,
        cached_key_value,
    )
    stream_f = stream.astype(jnp.float32)
    adapters = adapter_slot_table.shape[0]
    match = row_adapter_index[:, None] == jnp.arange(adapters)[None, :]
    slot = jnp.sum(jnp.where(match, adapter_slot_table[None, :], 0), axis=1)
    adapter_rank_value = jnp.sum(jnp.where(match, adapter_rank_table[None, :], 0), axis=1)
    owner = slot // kept_factors
    within = slot - owner * kept_factors
    target = (owner[:, None] == jnp.arange(stores)[None, :]).astype(jnp.int32)
    before = jnp.cumsum(target, axis=0) - target
    bucket = owner * capacity + jnp.sum(before * target, axis=1)
    packer = (bucket[None, :] == jnp.arange(stores * capacity)[:, None]).astype(jnp.bfloat16)
    outgoing = jnp.dot(packer, mixed, preferred_element_type=jnp.float32).astype(jnp.bfloat16)
    outgoing = outgoing.reshape(stores, capacity, -1)
    labels = jnp.stack(
        [(within + 1).astype(jnp.float32), adapter_rank_value.astype(jnp.float32)], axis=-1
    )
    labels = (
        jnp.dot(packer.astype(jnp.float32), labels)
        .astype(jnp.bfloat16)
        .reshape(stores, capacity, 2)
    )
    down_factor = adapter_down_weight.reshape(
        adapter_down_weight.shape[0], kept_factors * rank_padding
    )
    up_factor = adapter_up_weight.reshape(kept_factors * rank_padding, adapter_portion)
    block = lax.all_to_all(outgoing, "store", split_axis=0, concat_axis=0, tiled=True)
    marks = lax.all_to_all(labels, "store", split_axis=0, concat_axis=0, tiled=True)
    count = block.shape[0] * block.shape[1]
    flat = block.reshape(count, -1)
    code = marks[..., 0].reshape(count).astype(jnp.float32)
    row_rank_value = marks[..., 1].reshape(count).astype(jnp.float32)
    choose = code[:, None] - 1.0 == jnp.arange(kept_factors, dtype=jnp.float32)[None, :]
    gather_places = jnp.dot(flat, down_factor, preferred_element_type=jnp.float32).reshape(
        count, kept_factors, rank_padding
    )
    gather_places = jnp.sum(gather_places * choose.astype(jnp.float32)[:, :, None], axis=1)
    gather_places = lax.psum(gather_places, "tensor")
    live_positions = (
        jnp.arange(rank_padding, dtype=jnp.float32)[None, :] < row_rank_value[:, None]
    ).astype(jnp.float32)
    narrow_input = (
        gather_places
        * live_positions
        * (adapter_strength / jnp.maximum(row_rank_value, 1.0))[:, None]
    ).astype(jnp.bfloat16)
    rank_spread = (narrow_input[:, None, :] * choose.astype(jnp.bfloat16)[:, :, None]).reshape(
        count, kept_factors * rank_padding
    )
    narrow_output = jnp.dot(rank_spread, up_factor, preferred_element_type=jnp.float32).astype(
        jnp.bfloat16
    )
    narrow_output = narrow_output.reshape(block.shape[0], block.shape[1], adapter_portion)
    returned = lax.all_to_all(narrow_output, "store", split_axis=0, concat_axis=0, tiled=True)
    low_home = lax.dot_general(
        packer,
        returned.reshape(stores * capacity, adapter_portion),
        (((0,), (0,)), ((), ())),
        preferred_element_type=jnp.float32,
    )
    partial_sum = jnp.dot(mixed, output_projection, preferred_element_type=jnp.float32)
    gain = output_norm_gain.astype(jnp.float32)
    stream_mine = lax.dynamic_slice_in_dim(stream_f, column * adapter_portion, adapter_portion, 1)
    piece = (
        lax.dynamic_slice_in_dim(partial_sum, column * adapter_portion, adapter_portion, 1)
        + low_home
    )
    summand = lax.dynamic_update_slice_in_dim(partial_sum, piece, column * adapter_portion, 1)
    projected = lax.psum(summand, "tensor")
    mean = jnp.mean(projected * projected, axis=-1, keepdims=True)
    mine = lax.dynamic_slice_in_dim(projected, column * adapter_portion, adapter_portion, 1)
    return (stream_mine + mine * lax.rsqrt(mean + epsilon) * gain).astype(jnp.bfloat16)


def solution(mesh):
    in_specs = (
        P(("groups", "store"), None),
        P(),
        P("tensor"),
        P(None, "tensor"),
        P(None, None, "tensor"),
        P("tensor", None),
        P(None, ("groups", "store"), "tensor", None, None),
        P(("groups", "store")),
        P(("groups", "store")),
        P("groups"),
        P("groups"),
        P("tensor", ("groups", "store"), None),
        P(("groups", "store"), None, "tensor"),
    )
    out_specs = P(("groups", "store"), "tensor")
    return jax.shard_map(
        per_device, mesh=mesh, in_specs=in_specs, out_specs=out_specs, check_vma=False
    )
```
